32 devices in a mesh: row: 4 (over y, core), col: 8 (over z, x).
Axes of the slice: x: 2, y: 2, z: 4, core: 2. Of those that a mesh axis runs over, the one named last changes fastest.
Arguments:
- left_blocks: bfloat16 [4, 8, 2, 8, 64, 64], P('row', 'col'), may hold values from -0.375 to 0.375
- left_cols: int32 [4, 8, 2, 8], P('row', 'col'), may hold values from 0 to 15, all different within a row
- right_blocks: bfloat16 [4, 8, 16, 6, 64, 64], P('row', 'col'), may hold values from -6 to 6
- right_cols: int32 [4, 8, 16, 6], P('row', 'col'), may hold values from 0 to 15, all different within a row
- out_cols: int32 [4, 8, 2, 8], P('row', 'col'), may hold values from 0 to 15, all different within a row
Outputs:
- product: float32 [4, 8, 2, 8, 64, 64], P('row', 'col')
The draws below stay inside these ranges and needn't reach their ends.
Inputs may be any that keep to these rules, and one draw needn't show every extreme that they name: `left_cols`: the entries of one block row are distinct. `right_cols`: the entries of one block row are distinct. `out_cols`: the entries of one block row are distinct.
All inputs are finite; a program needn't handle non-finite values.
Results may differ from the reference program's by a relative error of at most 0.0003.
Values may be sent and summed in bfloat16 or wider, within the bound.
No kernel may reach another device: no remote copies, remote signals or barrier semaphores. Data moves between devices by JAX's collectives and lax.ppermute only.
A program may use at most 64 MiB of HBM per device.

```python
import jax
import jax.numpy as jnp
from jax import lax

BS = 64
IB = 2
KB = 16
JB = 16
NL = 8
NR = 6
NO = 8
TICKS = 8
N_ROW = 4
N_COL = 8


def level_of(own_key, shape, cuts, least, high):
    gain = 1.0
    for dim, parts in cuts:
        draws = jax.random.uniform(jax.random.fold_in(jax.random.fold_in(own_key, 6), dim), (parts,), jnp.float32, least / len(cuts), high / len(cuts))
        gain = gain * jnp.repeat(jnp.exp(draws), shape[dim] // parts).reshape((-1,) + (1,) * (len(shape) - 1 - dim))
    return gain


def picks_of(rng, rows, number_of, top, lift):
    sequence = jax.random.permutation(jax.random.fold_in(rng, 1), number_of)
    boost = sequence
    for power in range(3):
        boost = boost * boost // number_of
    boost = boost * lift // number_of
    chance = jax.random.randint(jax.random.fold_in(rng, 2), (rows, number_of), 0, 4096) + boost
    sure = jax.random.permutation(jax.random.fold_in(rng, 3), rows)[jnp.arange(number_of) % rows]
    chance = jnp.where(jnp.arange(rows)[:, None] == sure[None, :], 1 << 14, chance)
    score = chance * number_of + jnp.arange(number_of)
    return lax.top_k(score.astype(jnp.int32), top)[1].astype(jnp.int32)


def bell_draw(key, shape, spread, limit, pieces=(), kind=jnp.bfloat16):
    entries = spread * jax.random.normal(key, shape, jnp.float32)
    if pieces:
        entries = entries * level_of(key, shape, pieces, -0.22, 0.18)
    return jnp.clip(entries, -limit, limit).astype(kind)


def setup_inputs(seed: int = 0) -> dict:
    key_list = jax.random.split(jax.random.key(seed), 6)
    return {
        "left_blocks": bell_draw(key_list[0], (N_ROW, N_COL, IB, NL, BS, BS), (BS * 4) ** -0.5, 0.375, ((0, 4), (1, 8))),
        "left_cols": picks_of(key_list[1], N_ROW * N_COL * IB, KB, NL, 0).reshape((N_ROW, N_COL, IB, NL)),
        "right_blocks": bell_draw(key_list[2], (N_ROW, N_COL, KB, NR, BS, BS), 1.0, 6.0, ((0, 4), (1, 8))),
        "right_cols": picks_of(key_list[3], N_ROW * N_COL * KB, JB, NR, 0).reshape((N_ROW, N_COL, KB, NR)),
        "out_cols": picks_of(key_list[4], N_ROW * N_COL * IB, JB, NO, 0).reshape((N_ROW, N_COL, IB, NO)),
    }


def one_tick(left, left_cols, right, right_cols, pattern):
    inner = right.shape[0]
    pick_row = (left_cols[:, :, None] == jnp.arange(inner, dtype=jnp.int32)[None, None, :]).astype(jnp.float32)
    match = (right_cols[None, None, :, :] == pattern[:, :, None, None]).astype(jnp.float32)
    select = jnp.einsum('iak,iokb->iaokb', pick_row, match).astype(jnp.bfloat16)
    chosen = jnp.einsum('iaokb,kbyz->iaoyz', select, right, preferred_element_type=jnp.float32).astype(jnp.bfloat16)
    return jnp.einsum('iaxy,iaoyz->ioxz', left, chosen, preferred_element_type=jnp.float32)


def reference(left_blocks, left_cols, right_blocks, right_cols, out_cols):
    def panel(flat):
        row_index = flat // N_COL
        col_index = flat % N_COL
        total = jnp.zeros((IB, NO, BS, BS), jnp.float32)
        for step in range(TICKS):
            source_row = ((row_index - step) % N_ROW).astype(jnp.int32)
            source_col = ((col_index - TICKS + 1 + step) % N_COL).astype(jnp.int32)
            total = total + one_tick(left_blocks[source_row, source_col], left_cols[source_row, source_col], right_blocks[row_index, source_col], right_cols[row_index, source_col], out_cols[row_index, col_index])
        return total
    panels = lax.map(panel, jnp.arange(N_ROW * N_COL, dtype=jnp.int32))
    return panels.reshape(N_ROW, N_COL, IB, NO, BS, BS)
```

```python
import functools

import jax
import jax.numpy as jnp
from jax import lax
from jax.experimental import pallas as pl
from jax.experimental.pallas import tpu as pltpu
from jax.sharding import PartitionSpec as P

TICKS = 8
LANES = 128
PAD = 16
TOP = 32767.0
GRAIN = 8192.0


def shifted(value, axis, steps):
    count = lax.axis_size(axis)
    pairs = [(source, (source + steps) % count) for source in range(count)]
    return lax.ppermute(value, axis, pairs)


def one_tick(left, left_cols, right, right_cols, pattern):
    inner = right.shape[0]
    pick_row = (left_cols[:, :, None] == jnp.arange(inner, dtype=jnp.int32)[None, None, :]).astype(
        jnp.float32
    )
    match = (right_cols[None, None, :, :] == pattern[:, :, None, None]).astype(jnp.float32)
    select = jnp.einsum("iak,iokb->iaokb", pick_row, match).astype(jnp.bfloat16)
    chosen = jnp.einsum(
        "iaokb,kbyz->iaoyz", select, right, preferred_element_type=jnp.float32
    ).astype(jnp.bfloat16)
    return jnp.einsum("iaxy,iaoyz->ioxz", left, chosen, preferred_element_type=jnp.float32)


def ring(left_blocks, left_cols, right_blocks, right_cols, out_cols):
    left = left_blocks[0, 0]
    left_index = left_cols[0, 0]
    right = right_blocks[0, 0]
    right_index = right_cols[0, 0]
    pattern = out_cols[0, 0]
    total = jnp.zeros((left.shape[0], pattern.shape[1], left.shape[2], left.shape[3]), jnp.float32)
    carried = shifted(pattern, "col", 1 - TICKS)
    for step in range(TICKS):
        total = total + one_tick(left, left_index, right, right_index, carried)
        if step + 1 < TICKS:
            total, carried = shifted((total, carried), "col", 1)
            left, left_index = shifted((left, left_index), "row", 1)
    return total[None, None]


def encode(value, code_ref, lanes):
    rows = value.shape[0]
    peak = jnp.maximum(jnp.max(jnp.abs(value), axis=0, keepdims=True), 2.0**-100)
    power = jnp.floor(jnp.log2(peak))
    grains = jnp.ceil(peak * jnp.exp2(-power) * GRAIN) + 1.0
    factor = (TOP * GRAIN / grains) * jnp.exp2(-power)
    code_ref[:rows, lanes] = jnp.round(value * factor).astype(jnp.int32).astype(jnp.int16)
    row = lax.broadcasted_iota(jnp.int32, (PAD, value.shape[1]), 0)
    scale = jnp.where(row == 0, power, grains).astype(jnp.int32)
    code_ref[rows:, lanes] = scale.astype(jnp.int16)


def decode(code_ref, lanes, rows):
    power = code_ref[rows : rows + PAD, lanes].astype(jnp.int32).astype(jnp.float32)
    scale = jnp.exp2(power[:1]) * (power[1:2] * (1.0 / (TOP * GRAIN)))
    return code_ref[:rows, lanes].astype(jnp.int32).astype(jnp.float32) * scale


def spread_left(packed_ref, rows, half, pairs, dense_ref):
    blocks = packed_ref.shape[1] // LANES
    for i in range(rows // half):
        index = packed_ref[rows : rows + PAD, :].astype(jnp.float32)[i : i + 1, :].astype(jnp.int32)
        side = lax.broadcasted_iota(jnp.int32, (1, LANES), 1) // half
        here, there = [], []
        for b in range(blocks):
            column = index[:, b * LANES : (b + 1) * LANES]
            here.append(column - side)
            there.append(pltpu.roll(column, half, 1) - side)
        data = [
            packed_ref[i * half : (i + 1) * half, b * LANES : (b + 1) * LANES].astype(jnp.float32)
            for b in range(blocks)
        ]
        turned = [pltpu.roll(d, half, 1) for d in data]
        for m in range(pairs):
            total = jnp.zeros((half, LANES), jnp.float32)
            for b in range(blocks):
                total = jnp.where(here[b] == 2 * m, data[b], total)
                total = jnp.where(there[b] == 2 * m, turned[b], total)
            dense_ref[i * half : (i + 1) * half, m * LANES : (m + 1) * LANES] = total.astype(
                jnp.bfloat16
            )


def spread_right(cols_ref, right_ref, dense_ref):
    _, _, kb, kept, half, _ = right_ref.shape
    pairs = dense_ref.shape[1] // LANES
    side = lax.broadcasted_iota(jnp.int32, (half, LANES), 1) // half
    for k in range(kb):
        blocks = []
        for e in range(kept):
            block = right_ref[0, 0, k, e].astype(jnp.float32)
            blocks.append((jnp.concatenate([block, block], axis=1), cols_ref[0, 0, k, e]))
        for m in range(pairs):
            total = jnp.zeros((half, LANES), jnp.float32)
            for block, col in blocks:
                total = jnp.where(side == col - 2 * m, block, total)
            dense_ref[k * half : (k + 1) * half, m * LANES : (m + 1) * LANES] = total.astype(
                jnp.bfloat16
            )


def first_kernel(cols_ref, right_ref, packed_ref, dense_ref, code_ref, left_ref):
    rows = left_ref.shape[0]
    half = right_ref.shape[4]
    spread_right(cols_ref, right_ref, dense_ref)
    spread_left(packed_ref, rows, half, dense_ref.shape[0] // LANES, left_ref)
    part = jnp.dot(left_ref[...], dense_ref[...], preferred_element_type=jnp.float32)
    encode(part, code_ref, slice(None))


def second_kernel(half, dense_ref, packed_ref, code_ref, left_ref):
    rows = left_ref.shape[0]
    spread_left(packed_ref, rows, half, left_ref.shape[1] // LANES, left_ref)
    part = jnp.dot(left_ref[...], dense_ref[...], preferred_element_type=jnp.float32)
    encode(part, code_ref, slice(None))


def kept_kernel(half, dense_ref, near_ref, far_ref, a_ref, b_ref, left_ref):
    rows = a_ref.shape[0]
    pairs = left_ref.shape[1] // LANES
    spread_left(near_ref, rows, half, pairs, left_ref.at[:rows])
    spread_left(far_ref, rows, half, pairs, left_ref.at[rows:])
    part = jnp.dot(left_ref[...], dense_ref[...], preferred_element_type=jnp.float32)
    swap = (lax.axis_index("col") % 2) != (lax.axis_index("row") % 2)

    @pl.when(swap)
    def _():
        a_ref[...] = part[rows:]
        b_ref[...] = part[:rows]

    @pl.when(jnp.logical_not(swap))
    def _():
        a_ref[...] = part[:rows]
        b_ref[...] = part[rows:]


def sum_kernel(half, odd, own_ref, one_ref, two_ref, three_ref, kept_ref, code_ref, a_ref, b_ref, wide_ref, out_ref):
    rows, width = kept_ref.shape
    pairs = width // LANES
    for m in range(pairs):
        lanes = slice(m * LANES, (m + 1) * LANES)
        total = kept_ref[:, lanes] + decode(code_ref, lanes, rows)
        wide_ref[m] = total
        wide_ref[pairs + m] = pltpu.roll(total, half, 1)
    even = (lax.axis_index("col") % 2) == odd
    low = lax.broadcasted_iota(jnp.int32, (half, LANES), 1) < half
    count = own_ref.shape[3]
    for first, second, target in ((two_ref, one_ref, a_ref), (own_ref, three_ref, b_ref)):
        for o in range(0, count, 2):
            for i in range(rows // half):
                picked = []
                for side in range(2):
                    j = jnp.where(even, first[0, 0, i, o + side], second[0, 0, i, o + side])
                    slot = j // 2 + pairs * ((j + side) % 2)
                    picked.append(wide_ref[slot, i * half : (i + 1) * half, :])
                out_ref[i * half : (i + 1) * half, :] = jnp.where(low, picked[0], picked[1])
            lanes = slice(o // 2 * LANES, (o // 2 + 1) * LANES)
            encode(out_ref[...], target, lanes)


def last_kernel(half, a_ref, b_ref, c_ref, d_ref, out_ref):
    rows = a_ref.shape[0] - PAD
    for m in range(a_ref.shape[1] // LANES):
        lanes = slice(m * LANES, (m + 1) * LANES)
        total = decode(a_ref, lanes, rows) + decode(b_ref, lanes, rows)
        total = total + decode(c_ref, lanes, rows) + decode(d_ref, lanes, rows)
        for i in range(rows // half):
            part = total[i * half : (i + 1) * half]
            out_ref[0, 0, i, 2 * m] = part[:, :half]
            out_ref[0, 0, i, 2 * m + 1] = part[:, half:]


VMEM = pl.BlockSpec(memory_space=pltpu.VMEM)
SMEM = pl.BlockSpec(memory_space=pltpu.SMEM)
PARAMS = pltpu.CompilerParams(vmem_limit_bytes=40 * 2**20)


def grid_path(n_row, n_col, left_blocks, left_cols, right_blocks, right_cols, out_cols):
    _, _, ib, nl, bs, _ = left_blocks.shape
    kb = right_blocks.shape[2]
    jb = kb
    no = out_cols.shape[3]
    rows = ib * bs

    def send(value, to):
        pairs = []
        for r in range(n_row):
            for c in range(n_col):
                target = to(r, c)
                pairs.append((r * n_col + c, target[0] * n_col + target[1]))
        return lax.ppermute(value, ("row", "col"), pairs)

    def along(even, odd):
        return lambda r, c: (r, (c + 2 * (odd if c % 2 else even)) % n_col)

    packed = left_blocks[0, 0].transpose(0, 2, 1, 3).reshape(rows, nl * bs)
    index = jnp.repeat(left_cols[0, 0].astype(jnp.bfloat16), bs, axis=1)
    packed = jnp.concatenate([packed, index, jnp.zeros((PAD - ib, nl * bs), jnp.bfloat16)], axis=0)
    across = send(packed, lambda r, c: ((r + 2) % n_row, c))
    near = send(packed, lambda r, c: (r ^ 1, c))
    code = jax.ShapeDtypeStruct((rows + PAD, jb * bs), jnp.int16)
    small = jax.ShapeDtypeStruct((rows + PAD, no * bs), jnp.int16)
    wide = jax.ShapeDtypeStruct((rows, jb * bs), jnp.float32)
    left_scratch = pltpu.VMEM((rows, kb * bs), jnp.bfloat16)
    dense, code_one = pl.pallas_call(
        first_kernel,
        out_shape=(jax.ShapeDtypeStruct((kb * bs, jb * bs), jnp.bfloat16), code),
        in_specs=[SMEM, VMEM, VMEM],
        out_specs=(VMEM, VMEM),
        scratch_shapes=[left_scratch],
        compiler_params=PARAMS,
        name="first",
    )(right_cols, right_blocks, packed)
    got_one = send(code_one, lambda r, c: (r, c ^ 1))
    far = send(across, lambda r, c: (r ^ 1, c))
    code_two = pl.pallas_call(
        functools.partial(second_kernel, bs),
        out_shape=code,
        in_specs=[VMEM, VMEM],
        out_specs=VMEM,
        scratch_shapes=[left_scratch],
        compiler_params=PARAMS,
        name="second",
    )(dense, across)
    got_two = send(code_two, lambda r, c: (r, c ^ 1))
    kept_a, kept_b = pl.pallas_call(
        functools.partial(kept_kernel, bs),
        out_shape=(wide, wide),
        in_specs=[VMEM] * 3,
        out_specs=(VMEM, VMEM),
        scratch_shapes=[pltpu.VMEM((2 * rows, kb * bs), jnp.bfloat16)],
        compiler_params=PARAMS,
        name="kept",
    )(dense, near, far)
    pattern = [send(out_cols, along(-d, -d)) for d in (1, 2, -1)]

    def summed(odd, kept, code):
        return pl.pallas_call(
            functools.partial(sum_kernel, bs, odd),
            out_shape=(small, small),
            in_specs=[SMEM] * 4 + [VMEM] * 2,
            out_specs=(VMEM, VMEM),
            scratch_shapes=[
                pltpu.VMEM((2 * (jb * bs // LANES), rows, LANES), jnp.float32),
                pltpu.VMEM((rows, LANES), jnp.float32),
            ],
            compiler_params=PARAMS,
            name="sum",
        )(out_cols, *pattern, kept, code)

    a, b = summed(0, kept_a, got_one)
    got = [send(a, along(2, 1)), send(b, along(0, -1))]
    a, b = summed(1, kept_b, got_two)
    got += [send(a, along(1, 2)), send(b, along(-1, 0))]
    return pl.pallas_call(
        functools.partial(last_kernel, bs),
        out_shape=jax.ShapeDtypeStruct((1, 1, ib, no, bs, bs), jnp.float32),
        in_specs=[VMEM] * 4,
        out_specs=VMEM,
        compiler_params=PARAMS,
        name="last",
    )(*got)


def solution(mesh):
    in_specs = (
        P("row", "col", None, None, None, None),
        P("row", "col", None, None),
        P("row", "col", None, None, None, None),
        P("row", "col", None, None),
        P("row", "col", None, None),
    )
    out_specs = P("row", "col", None, None, None, None)
    n_row, n_col = mesh.shape["row"], mesh.shape["col"]
    body = functools.partial(grid_path, n_row, n_col) if (n_row, n_col) == (4, TICKS) else ring
    return jax.shard_map(body, mesh=mesh, in_specs=in_specs, out_specs=out_specs, check_vma=False)
```

```python
import functools

import jax
import jax.numpy as jnp
from jax import lax
from jax.experimental import pallas as pl
from jax.experimental.pallas import tpu as pltpu
from jax.sharding import PartitionSpec as P

TICKS = 8
LANES = 128
PAD = 16
TOP = 32767.0
GRAIN = 8192.0


def shifted(value, axis, steps):
    count = lax.axis_size(axis)
    pairs = [(source, (source + steps) % count) for source in range(count)]
    return lax.ppermute(value, axis, pairs)


def one_tick(left, left_cols, right, right_cols, pattern):
    inner = right.shape[0]
    pick_row = (left_cols[:, :, None] == jnp.arange(inner, dtype=jnp.int32)[None, None, :]).astype(
        jnp.float32
    )
    match = (right_cols[None, None, :, :] == pattern[:, :, None, None]).astype(jnp.float32)
    select = jnp.einsum("iak,iokb->iaokb", pick_row, match).astype(jnp.bfloat16)
    chosen = jnp.einsum(
        "iaokb,kbyz->iaoyz", select, right, preferred_element_type=jnp.float32
    ).astype(jnp.bfloat16)
    return jnp.einsum("iaxy,iaoyz->ioxz", left, chosen, preferred_element_type=jnp.float32)


def ring(left_blocks, left_cols, right_blocks, right_cols, out_cols):
    left = left_blocks[0, 0]
    left_index = left_cols[0, 0]
    right = right_blocks[0, 0]
    right_index = right_cols[0, 0]
    pattern = out_cols[0, 0]
    total = jnp.zeros((left.shape[0], pattern.shape[1], left.shape[2], left.shape[3]), jnp.float32)
    carried = shifted(pattern, "col", 1 - TICKS)
    for step in range(TICKS):
        total = total + one_tick(left, left_index, right, right_index, carried)
        if step + 1 < TICKS:
            total, carried = shifted((total, carried), "col", 1)
            left, left_index = shifted((left, left_index), "row", 1)
    return total[None, None]


def encode(parts, code_ref):
    rows = parts[0].shape[0]
    row = lax.broadcasted_iota(jnp.int32, (PAD, LANES), 0)
    scales = jnp.zeros((PAD, LANES), jnp.float32)
    for m, value in enumerate(parts):
        peak = jnp.maximum(jnp.max(jnp.abs(value), axis=0, keepdims=True), 2.0**-100)
        power = jnp.floor(jnp.log2(peak))
        shrink = jnp.exp2(-power)
        grains = jnp.ceil(peak * shrink * GRAIN) + 1.0
        factor = (TOP * GRAIN / grains) * shrink
        code_ref[m * rows : (m + 1) * rows] = jnp.round(value * factor).astype(jnp.int16)
        scales = jnp.where(row == m, power, jnp.where(row == PAD // 2 + m, grains, scales))
    code_ref[len(parts) * rows :] = scales.astype(jnp.int16)


def decoded(code_ref, rows):
    count = code_ref.shape[0] // rows
    tile = code_ref[count * rows :].astype(jnp.float32)
    scales = jnp.exp2(tile[: PAD // 2]) * (tile[PAD // 2 :] * (1.0 / (TOP * GRAIN)))
    for m in range(count):
        yield code_ref[m * rows : (m + 1) * rows].astype(jnp.float32) * scales[m : m + 1]


def spread_left(packed_ref, rows, half, dense_ref):
    side = lax.broadcasted_iota(jnp.int32, (1, LANES), 1) // half
    index = packed_ref[rows : rows + PAD, :].astype(jnp.float32)
    for i in range(rows // half):
        here, there, data, turned = [], [], [], []
        for b in range(packed_ref.shape[1] // LANES):
            lanes = slice(b * LANES, (b + 1) * LANES)
            column = index[i : i + 1, lanes].astype(jnp.int32)
            here.append(jnp.broadcast_to(column - side, (PAD, LANES)))
            there.append(jnp.broadcast_to(pltpu.roll(column, half, 1) - side, (PAD, LANES)))
            data.append(packed_ref[i * half : (i + 1) * half, lanes])
            turned.append(pltpu.roll(data[-1], half, 1))
        for m in range(dense_ref.shape[1] // LANES):
            masks = [(h == 2 * m, t == 2 * m) for h, t in zip(here, there)]
            for top in range(0, half, PAD):
                total = jnp.zeros((PAD, LANES), jnp.bfloat16)
                for b, (stays, turns) in enumerate(masks):
                    total = jnp.where(stays, data[b][top : top + PAD], total)
                    total = jnp.where(turns, turned[b][top : top + PAD], total)
                rows_of = slice(i * half + top, i * half + top + PAD)
                dense_ref[rows_of, m * LANES : (m + 1) * LANES] = total


def product(left, dense_ref):
    found = []
    for m in range(0, dense_ref.shape[0], 2):
        pair = jnp.concatenate([dense_ref[m], dense_ref[m + 1]], axis=1)
        part = jnp.dot(left, pair, preferred_element_type=jnp.float32)
        found += [part[:, :LANES], part[:, LANES:]]
    return found


def place(blocks, dense_ref):
    half = blocks[0][0].shape[0]
    side = lax.broadcasted_iota(jnp.int32, (half, LANES), 1) // half
    work = []
    for block, row, col in blocks:
        both = jnp.concatenate([block.astype(jnp.float32)]*2, axis=1).astype(jnp.bfloat16)
        at = (lax.shift_right_logical(col, 1), slice(row * half, (row + 1) * half))
        work.append((at, jnp.where(side == (col & 1), both, dense_ref[at])))
    for at, value in work:
        dense_ref[at] = value


def first_kernel(
    right_cols_hbm,
    left_cols_hbm,
    left_hbm,
    right_hbm,
    dense_ref,
    code_ref,
    packed_ref,
    left_ref,
    right_cols_ref,
    left_cols_ref,
    left_raw,
    right_raw,
    sem,
):
    ib, nl, half, _ = left_raw.shape
    kb, kept, _, _ = right_raw.shape
    rows = ib * half
    parts = sem.shape[0] - 3
    step = kb // parts
    pairs = [(left_cols_hbm, left_cols_ref), (left_hbm.at[0, 0], left_raw), (right_cols_hbm, right_cols_ref)]
    for part in range(parts):
        here = pl.ds(part * step, step)
        pairs.append((right_hbm.at[0, 0, here], right_raw.at[here]))
    copies = [pltpu.make_async_copy(*pair, sem.at[n]) for n, pair in enumerate(pairs)]
    for copy in copies:
        copy.start()
    left_ref[...] = jnp.zeros_like(left_ref)
    dense_ref[...] = jnp.zeros_like(dense_ref)
    copies[0].wait()
    copies[1].wait()
    side = lax.broadcasted_iota(jnp.int32, (PAD, LANES), 1) // half
    row = lax.broadcasted_iota(jnp.int32, (PAD, LANES), 0)
    for b in range(nl // 2):
        lanes = slice(b * LANES, (b + 1) * LANES)
        index = jnp.zeros((PAD, LANES), jnp.int32)
        for i in range(ib):
            pair = jnp.concatenate([left_raw[i, 2 * b], left_raw[i, 2 * b + 1]], axis=1)
            packed_ref[i * half : (i + 1) * half, lanes] = pair
            cols = jnp.where(side == 0, left_cols_ref[0, 0, i, 2 * b], left_cols_ref[0, 0, i, 2 * b + 1])
            index = jnp.where(row == i, cols, index)
        packed_ref[rows:, lanes] = index.astype(jnp.float32).astype(jnp.bfloat16)
    for a in range(nl):
        place([(left_raw[i, a], i, left_cols_ref[0, 0, i, a]) for i in range(ib)], left_ref)
    copies[2].wait()
    for part in range(parts):
        copies[part + 3].wait()
        for e in range(kept):
            ks = range(part * step, (part + 1) * step)
            place([(right_raw[k, e], k, right_cols_ref[0, e, 0, k]) for k in ks], dense_ref)
    left = jnp.concatenate([left_ref[m] for m in range(left_ref.shape[0])], axis=1)
    encode(product(left, dense_ref), code_ref)


def second_kernel(half, dense_ref, packed_ref, own_cols_ref, one_cols_ref, *refs):
    *code_refs, pair_ref, left_ref = refs
    pair_ref[0] = own_cols_ref[0]
    pair_ref[1] = one_cols_ref[0]
    spread_left(packed_ref, left_ref.shape[0], half, left_ref)
    found = product(left_ref[...], dense_ref)
    for i, code_ref in enumerate(code_refs):
        encode([part[i * half : (i + 1) * half] for part in found], code_ref)


def swapped():
    return (lax.axis_index("col") + lax.axis_index("row")) % 2


def near_kernel(half, dense_ref, packed_ref, kept_ref, left_ref):
    spread_left(packed_ref, left_ref.shape[0], half, left_ref)
    slot = swapped()
    for m, part in enumerate(product(left_ref[...], dense_ref)):
        kept_ref[slot, m] = part


def far_kernel(half, dense_ref, packed_ref, _, kept_ref, left_ref):
    spread_left(packed_ref, left_ref.shape[0], half, left_ref)
    slot = 1 - swapped()
    for m, part in enumerate(product(left_ref[...], dense_ref)):
        kept_ref[slot, m] = part


def sum_kernel(half, odd, first, own_ref, one_ref, far_ref, kept_ref, code_ref, *refs):
    pairs = kept_ref.shape[1]
    rows = (code_ref.shape[0] - PAD) // pairs
    if odd:
        held_ref, a_ref, b_ref, keep_ref, wide_ref, new_ref = refs
        held_refs, new_refs = [held_ref], [new_ref]
    else:
        a_ref, *new_refs, wide_ref = refs
    for m, part in enumerate(decoded(code_ref, rows)):
        total = kept_ref[odd, m, first * half : first * half + rows] + part
        wide_ref[m] = total
        wide_ref[pairs + m] = pltpu.roll(total, half, 1)
    low = lax.broadcasted_iota(jnp.int32, (half, LANES), 1) < half
    stays = (lax.axis_index("col") % 2) == odd

    def pick(near, i, o):
        picked = []
        for side in range(2):
            at = (0, first + i, o + side)
            if near:
                j = jnp.where(stays, own_ref[(0, *at)], one_ref[(0, *at)])
            else:
                j = jnp.where(stays, far_ref[(0, *at)], far_ref[(1, *at)])
            slot = lax.shift_right_logical(j, 1) + pairs * ((j + side) & 1)
            picked.append(wide_ref[slot, i * half : (i + 1) * half, :])
        return jnp.where(low, picked[0], picked[1])

    count = own_ref.shape[3]
    blocks = range(rows // half)
    encode([jnp.concatenate([pick(False, i, o) for i in blocks], axis=0) for o in range(0, count, 2)], a_ref)
    for i, new_ref in zip(blocks, new_refs):
        encode([pick(True, i, o) for o in range(0, count, 2)], new_ref)
    if odd:
        b_ref[...] = jnp.where(stays, held_ref[...], new_ref[...])
        keep_ref[...] = jnp.where(stays, new_ref[...], held_ref[...])


def last_kernel(half, whole_ref, *refs):
    *part_refs, out_ref = refs
    ib = out_ref.shape[2]
    parts = [[decoded(ref, half) for ref in part_refs[i::ib]] for i in range(ib)]
    for m, whole in enumerate(decoded(whole_ref, ib * half)):
        for i in range(ib):
            total = whole[i * half : (i + 1) * half]
            for part in parts[i]:
                total = total + next(part)
            out_ref[0, 0, i, 2 * m] = total[:, :half]
            out_ref[0, 0, i, 2 * m + 1] = total[:, half:]


VMEM = pl.BlockSpec(memory_space=pltpu.VMEM)
SMEM = pl.BlockSpec(memory_space=pltpu.SMEM)
HBM = pl.BlockSpec(memory_space=pltpu.HBM)
PARTS = 4
PARAMS = pltpu.CompilerParams(vmem_limit_bytes=40 * 2**20)


def grid_path(n_row, n_col, left_blocks, left_cols, right_blocks, right_cols, out_cols):
    _, _, ib, nl, bs, _ = left_blocks.shape
    kb = right_blocks.shape[2]
    jb = kb
    no = out_cols.shape[3]
    rows = ib * bs

    def send(value, to):
        pairs = []
        for r in range(n_row):
            for c in range(n_col):
                target = to(r, c)
                pairs.append((r * n_col + c, target[0] * n_col + target[1]))
        return lax.ppermute(value, ("row", "col"), pairs)

    def along(even, odd):
        return lambda r, c: (r, c ^ (2 * (odd if c % 2 else even)))

    wide_cols, no_cols = jb * bs // LANES, no * bs // LANES
    code = jax.ShapeDtypeStruct((wide_cols * rows + PAD, LANES), jnp.int16)
    code_part = jax.ShapeDtypeStruct((wide_cols * bs + PAD, LANES), jnp.int16)
    small = jax.ShapeDtypeStruct((no_cols * rows + PAD, LANES), jnp.int16)
    small_part = jax.ShapeDtypeStruct((no_cols * bs + PAD, LANES), jnp.int16)
    both = jax.ShapeDtypeStruct((2, wide_cols, rows, LANES), jnp.float32)
    left_scratch = pltpu.VMEM((rows, kb * bs), jnp.bfloat16)
    operands = (right_cols.transpose(0, 3, 1, 2), left_cols, left_blocks, right_blocks)
    dense, code_one, packed = pl.pallas_call(
        first_kernel,
        out_shape=(
            jax.ShapeDtypeStruct((wide_cols, kb * bs, LANES), jnp.bfloat16),
            code,
            jax.ShapeDtypeStruct((rows + PAD, nl * bs), jnp.bfloat16),
        ),
        in_specs=[HBM] * 4,
        out_specs=(VMEM, VMEM, VMEM),
        scratch_shapes=[
            pltpu.VMEM((kb * bs // LANES, rows, LANES), jnp.bfloat16),
            pltpu.SMEM((1, right_cols.shape[3], 1, kb), jnp.int32),
            pltpu.SMEM(left_cols.shape[:2] + (ib, nl), jnp.int32),
            pltpu.VMEM(left_blocks.shape[2:], jnp.bfloat16),
            pltpu.VMEM(right_blocks.shape[2:], jnp.bfloat16),
            pltpu.SemaphoreType.DMA((PARTS + 3,)),
        ],
        compiler_params=PARAMS,
        name="first",
    )(*(pltpu.with_memory_space_constraint(a, pltpu.HBM) for a in operands))
    got_one = send(code_one, lambda r, c: (r, c ^ 1))
    across = send(packed, lambda r, c: ((r + 2) % n_row, c))
    near = send(packed, lambda r, c: (r ^ 1, c))
    kept = pl.pallas_call(
        functools.partial(near_kernel, bs),
        out_shape=both,
        in_specs=[VMEM, VMEM],
        out_specs=VMEM,
        scratch_shapes=[left_scratch],
        compiler_params=PARAMS,
        name="near",
    )(dense, near)
    kept, own_cols = lax.optimization_barrier((kept, out_cols))
    one_cols = send(own_cols, along(1, 1))
    across, kept, one_cols = lax.optimization_barrier((across, kept, one_cols))
    far = send(across, lambda r, c: (r ^ 1, c))
    *codes, pair_cols = pl.pallas_call(
        functools.partial(second_kernel, bs),
        out_shape=(*(ib * (code_part,)), jax.ShapeDtypeStruct((2, *out_cols.shape[1:]), jnp.int32)),
        in_specs=[VMEM] * 4,
        out_specs=(ib + 1) * (VMEM,),
        scratch_shapes=[left_scratch],
        compiler_params=PARAMS,
        name="second",
    )(dense, across, own_cols, one_cols)
    got_two = [send(code, lambda r, c: (r, c ^ 1)) for code in codes]
    far_cols = send(pair_cols, along(2, 2))
    kept = pl.pallas_call(
        functools.partial(far_kernel, bs),
        out_shape=both,
        in_specs=[VMEM, VMEM, HBM],
        out_specs=VMEM,
        scratch_shapes=[left_scratch],
        input_output_aliases={2: 0},
        compiler_params=PARAMS,
        name="far",
    )(dense, far, kept)

    def summed(odd, first, code, *held):
        if odd:
            outs = 3 * (small_part,)
        else:
            outs = (small, *(ib * (small_part,)))
        scratch = [pltpu.VMEM((2 * wide_cols, rows if not odd else bs, LANES), jnp.float32)]
        scratch += odd * [pltpu.VMEM(small_part.shape, small_part.dtype)]
        return pl.pallas_call(
            functools.partial(sum_kernel, bs, odd, first),
            out_shape=outs,
            in_specs=[SMEM] * 3 + [VMEM] * (2 + odd),
            out_specs=len(outs) * (VMEM,),
            scratch_shapes=scratch,
            compiler_params=PARAMS,
            name="sum",
        )(own_cols, one_cols, far_cols, kept, code, *held)

    a, *held = summed(0, 0, got_one)
    whole = send(a, along(2, 3))
    parts = []
    for i in range(ib):
        a, b, keep = summed(1, i, got_two[i], held[i])
        parts.append((send(a, along(3, 2)), send(b, along(1, 1)), keep))
    got = [whole, *(part for group in zip(*parts) for part in group)]
    return pl.pallas_call(
        functools.partial(last_kernel, bs),
        out_shape=jax.ShapeDtypeStruct((1, 1, ib, no, bs, bs), jnp.float32),
        in_specs=[VMEM] * len(got),
        out_specs=VMEM,
        compiler_params=PARAMS,
        name="last",
    )(*got)


def solution(mesh):
    in_specs = (
        P("row", "col", None, None, None, None),
        P("row", "col", None, None),
        P("row", "col", None, None, None, None),
        P("row", "col", None, None),
        P("row", "col", None, None),
    )
    out_specs = P("row", "col", None, None, None, None)
    n_row, n_col = mesh.shape["row"], mesh.shape["col"]
    body = functools.partial(grid_path, n_row, n_col) if (n_row, n_col) == (4, TICKS) else ring
    return jax.shard_map(body, mesh=mesh, in_specs=in_specs, out_specs=out_specs, check_vma=False)
```

```python
import functools

import jax
import jax.numpy as jnp
from jax import lax
from jax.experimental import pallas as pl
from jax.experimental.pallas import tpu as pltpu
from jax.sharding import PartitionSpec as P

TICKS = 8
LANES = 128
PAD = 16
TOP = 32767.0
GRAIN = 8192.0


def shifted(value, axis, steps):
    count = lax.axis_size(axis)
    pairs = [(source, (source + steps) % count) for source in range(count)]
    return lax.ppermute(value, axis, pairs)


def one_tick(left, left_cols, right, right_cols, pattern):
    inner = right.shape[0]
    pick_row = (left_cols[:, :, None] == jnp.arange(inner, dtype=jnp.int32)[None, None, :]).astype(
        jnp.float32
    )
    match = (right_cols[None, None, :, :] == pattern[:, :, None, None]).astype(jnp.float32)
    select = jnp.einsum("iak,iokb->iaokb", pick_row, match).astype(jnp.bfloat16)
    chosen = jnp.einsum(
        "iaokb,kbyz->iaoyz", select, right, preferred_element_type=jnp.float32
    ).astype(jnp.bfloat16)
    return jnp.einsum("iaxy,iaoyz->ioxz", left, chosen, preferred_element_type=jnp.float32)


def ring(left_blocks, left_cols, right_blocks, right_cols, out_cols):
    left = left_blocks[0, 0]
    left_index = left_cols[0, 0]
    right = right_blocks[0, 0]
    right_index = right_cols[0, 0]
    pattern = out_cols[0, 0]
    total = jnp.zeros((left.shape[0], pattern.shape[1], left.shape[2], left.shape[3]), jnp.float32)
    carried = shifted(pattern, "col", 1 - TICKS)
    for step in range(TICKS):
        total = total + one_tick(left, left_index, right, right_index, carried)
        if step + 1 < TICKS:
            total, carried = shifted((total, carried), "col", 1)
            left, left_index = shifted((left, left_index), "row", 1)
    return total[None, None]


def encode(parts, code_ref):
    rows = parts[0].shape[0]
    row = lax.broadcasted_iota(jnp.int32, (PAD, LANES), 0)
    scales = jnp.zeros((PAD, LANES), jnp.float32)
    for m, value in enumerate(parts):
        peak = jnp.maximum(jnp.max(jnp.abs(value), axis=0, keepdims=True), 2.0**-100)
        power = jnp.floor(jnp.log2(peak))
        shrink = jnp.exp2(-power)
        grains = jnp.ceil(peak * shrink * GRAIN) + 1.0
        factor = (TOP * GRAIN / grains) * shrink
        code_ref[m * rows : (m + 1) * rows] = jnp.round(value * factor).astype(jnp.int16)
        scales = jnp.where(row == m, power, jnp.where(row == PAD // 2 + m, grains, scales))
    code_ref[len(parts) * rows :] = scales.astype(jnp.int16)


def decoded(code_ref, rows):
    count = code_ref.shape[0] // rows
    tile = code_ref[count * rows :].astype(jnp.float32)
    scales = jnp.exp2(tile[: PAD // 2]) * (tile[PAD // 2 :] * (1.0 / (TOP * GRAIN)))
    for m in range(count):
        yield code_ref[m * rows : (m + 1) * rows].astype(jnp.float32) * scales[m : m + 1]


def spread_left(packed_ref, rows, half, dense_ref):
    side = lax.broadcasted_iota(jnp.int32, (1, LANES), 1) // half
    index = packed_ref[rows : rows + PAD, :].astype(jnp.float32)
    for i in range(rows // half):
        here, there, data, turned = [], [], [], []
        for b in range(packed_ref.shape[1] // LANES):
            lanes = slice(b * LANES, (b + 1) * LANES)
            column = index[i : i + 1, lanes].astype(jnp.int32)
            here.append(jnp.broadcast_to(column - side, (PAD, LANES)))
            there.append(jnp.broadcast_to(pltpu.roll(column, half, 1) - side, (PAD, LANES)))
            data.append(packed_ref[i * half : (i + 1) * half, lanes])
            turned.append(pltpu.roll(data[-1], half, 1))
        for m in range(dense_ref.shape[1] // LANES):
            masks = [(h == 2 * m, t == 2 * m) for h, t in zip(here, there)]
            for top in range(0, half, PAD):
                total = jnp.zeros((PAD, LANES), jnp.bfloat16)
                for b, (stays, turns) in enumerate(masks):
                    total = jnp.where(stays, data[b][top : top + PAD], total)
                    total = jnp.where(turns, turned[b][top : top + PAD], total)
                rows_of = slice(i * half + top, i * half + top + PAD)
                dense_ref[rows_of, m * LANES : (m + 1) * LANES] = total


def product(left, dense_ref):
    found = []
    for m in range(0, dense_ref.shape[0], 2):
        pair = jnp.concatenate([dense_ref[m], dense_ref[m + 1]], axis=1)
        part = jnp.dot(left, pair, preferred_element_type=jnp.float32)
        found += [part[:, :LANES], part[:, LANES:]]
    return found


def place(blocks, dense_ref):
    half = blocks[0][0].shape[0]
    side = lax.broadcasted_iota(jnp.int32, (half, LANES), 1) // half
    work = []
    for block, row, col in blocks:
        both = jnp.concatenate([block.astype(jnp.float32)]*2, axis=1).astype(jnp.bfloat16)
        at = (lax.shift_right_logical(col, 1), slice(row * half, (row + 1) * half))
        work.append((at, jnp.where(side == (col & 1), both, dense_ref[at])))
    for at, value in work:
        dense_ref[at] = value


def pack_kernel(cols_hbm, left_hbm, packed_ref, cols_ref, left_ref, sem):
    ib, nl, half, _ = left_ref.shape
    rows = ib * half
    copies = [
        pltpu.make_async_copy(cols_hbm, cols_ref, sem.at[0]),
        pltpu.make_async_copy(left_hbm.at[0, 0], left_ref, sem.at[1]),
    ]
    for copy in copies:
        copy.start()
    side = lax.broadcasted_iota(jnp.int32, (PAD, LANES), 1) // half
    row = lax.broadcasted_iota(jnp.int32, (PAD, LANES), 0)
    copies[0].wait()
    for b in range(nl // 2):
        index = jnp.zeros((PAD, LANES), jnp.int32)
        for i in range(ib):
            cols = jnp.where(side == 0, cols_ref[0, 0, i, 2 * b], cols_ref[0, 0, i, 2 * b + 1])
            index = jnp.where(row == i, cols, index)
        packed_ref[rows:, b * LANES : (b + 1) * LANES] = index.astype(jnp.float32).astype(jnp.bfloat16)
    copies[1].wait()
    for b in range(nl // 2):
        for i in range(ib):
            pair = jnp.concatenate([left_ref[i, 2 * b], left_ref[i, 2 * b + 1]], axis=1)
            packed_ref[i * half : (i + 1) * half, b * LANES : (b + 1) * LANES] = pair


def first_kernel(cols_hbm, right_hbm, packed_ref, dense_ref, code_ref, left_ref, cols_ref, right_ref, sem):
    kb, kept, half, _ = right_ref.shape
    rows = left_ref.shape[0]
    parts = sem.shape[0] - 1
    step = kb // parts
    pairs = [(cols_hbm, cols_ref)]
    for part in range(parts):
        here = pl.ds(part * step, step)
        pairs.append((right_hbm.at[0, 0, here], right_ref.at[here]))
    copies = [pltpu.make_async_copy(*pair, sem.at[n]) for n, pair in enumerate(pairs)]
    for copy in copies:
        copy.start()
    dense_ref[...] = jnp.zeros_like(dense_ref)
    spread_left(packed_ref, rows, half, left_ref)
    copies[0].wait()
    for part in range(parts):
        copies[part + 1].wait()
        for e in range(kept):
            ks = range(part * step, (part + 1) * step)
            place([(right_ref[k, e], k, cols_ref[0, e, 0, k]) for k in ks], dense_ref)
    encode(product(left_ref[...], dense_ref), code_ref)


def second_kernel(half, dense_ref, packed_ref, code_ref, left_ref):
    spread_left(packed_ref, left_ref.shape[0], half, left_ref)
    encode(product(left_ref[...], dense_ref), code_ref)


def swapped():
    return (lax.axis_index("col") + lax.axis_index("row")) % 2


def near_kernel(half, dense_ref, packed_ref, kept_ref, left_ref):
    spread_left(packed_ref, left_ref.shape[0], half, left_ref)
    slot = swapped()
    for m, part in enumerate(product(left_ref[...], dense_ref)):
        kept_ref[slot, m] = part


def far_kernel(half, dense_ref, packed_ref, _, kept_ref, left_ref):
    spread_left(packed_ref, left_ref.shape[0], half, left_ref)
    slot = 1 - swapped()
    for m, part in enumerate(product(left_ref[...], dense_ref)):
        kept_ref[slot, m] = part


def sum_kernel(half, odd, own_ref, one_ref, far_ref, kept_ref, code_ref, *refs):
    if odd:
        held_ref, a_ref, b_ref, keep_ref, wide_ref, new_ref = refs
    else:
        a_ref, new_ref, wide_ref = refs
    _, pairs, rows, _ = kept_ref.shape
    for m, part in enumerate(decoded(code_ref, rows)):
        total = kept_ref[odd, m] + part
        wide_ref[m] = total
        wide_ref[pairs + m] = pltpu.roll(total, half, 1)
    low = lax.broadcasted_iota(jnp.int32, (half, LANES), 1) < half
    stays = (lax.axis_index("col") % 2) == odd

    def pick(near, i, o):
        picked = []
        for side in range(2):
            at = (0, 0, i, o + side)
            j = jnp.where(stays, own_ref[at], one_ref[at]) if near else far_ref[at]
            slot = lax.shift_right_logical(j, 1) + pairs * ((j + side) & 1)
            picked.append(wide_ref[slot, i * half : (i + 1) * half, :])
        return jnp.where(low, picked[0], picked[1])

    for near, target in ((False, a_ref), (True, new_ref)):
        steps = range(0, own_ref.shape[3], 2)
        encode([jnp.concatenate([pick(near, i, o) for i in range(rows // half)], axis=0) for o in steps], target)
    if odd:
        b_ref[...] = jnp.where(stays, held_ref[...], new_ref[...])
        keep_ref[...] = jnp.where(stays, new_ref[...], held_ref[...])


def last_kernel(half, a_ref, b_ref, c_ref, own_ref, out_ref):
    ib = out_ref.shape[2]
    arrived = [decoded(ref, ib * half) for ref in (a_ref, b_ref, c_ref, own_ref)]
    for m, (a, b, c, own) in enumerate(zip(*arrived)):
        total = (a + own) + (b + c)
        for i in range(ib):
            part = total[i * half : (i + 1) * half]
            out_ref[0, 0, i, 2 * m] = part[:, :half]
            out_ref[0, 0, i, 2 * m + 1] = part[:, half:]


VMEM = pl.BlockSpec(memory_space=pltpu.VMEM)
SMEM = pl.BlockSpec(memory_space=pltpu.SMEM)
HBM = pl.BlockSpec(memory_space=pltpu.HBM)
PARTS = 4
PARAMS = pltpu.CompilerParams(vmem_limit_bytes=40 * 2**20)


def grid_path(n_row, n_col, left_blocks, left_cols, right_blocks, right_cols, out_cols):
    _, _, ib, nl, bs, _ = left_blocks.shape
    kb = right_blocks.shape[2]
    jb = kb
    no = out_cols.shape[3]
    rows = ib * bs

    def send(value, to):
        pairs = []
        for r in range(n_row):
            for c in range(n_col):
                target = to(r, c)
                pairs.append((r * n_col + c, target[0] * n_col + target[1]))
        return lax.ppermute(value, ("row", "col"), pairs)

    def along(even, odd):
        return lambda r, c: (r, c ^ (2 * (odd if c % 2 else even)))

    wide_cols, no_cols = jb * bs // LANES, no * bs // LANES
    code = jax.ShapeDtypeStruct((wide_cols * rows + PAD, LANES), jnp.int16)
    small = jax.ShapeDtypeStruct((no_cols * rows + PAD, LANES), jnp.int16)
    both = jax.ShapeDtypeStruct((2, wide_cols, rows, LANES), jnp.float32)
    left_scratch = pltpu.VMEM((rows, kb * bs), jnp.bfloat16)
    def in_hbm(*arrays):
        return [pltpu.with_memory_space_constraint(array, pltpu.HBM) for array in arrays]

    packed = pl.pallas_call(
        pack_kernel,
        out_shape=jax.ShapeDtypeStruct((rows + PAD, nl * bs), jnp.bfloat16),
        in_specs=[HBM] * 2,
        out_specs=VMEM,
        scratch_shapes=[
            pltpu.SMEM(left_cols.shape[:2] + (ib, nl), jnp.int32),
            pltpu.VMEM(left_blocks.shape[2:], jnp.bfloat16),
            pltpu.SemaphoreType.DMA((2,)),
        ],
        compiler_params=PARAMS,
        name="pack",
    )(*in_hbm(left_cols, left_blocks))
    dense, code_one = pl.pallas_call(
        first_kernel,
        out_shape=(jax.ShapeDtypeStruct((wide_cols, kb * bs, LANES), jnp.bfloat16), code),
        in_specs=[HBM, HBM, VMEM],
        out_specs=(VMEM, VMEM),
        scratch_shapes=[
            left_scratch,
            pltpu.SMEM((1, right_cols.shape[3], 1, kb), jnp.int32),
            pltpu.VMEM(right_blocks.shape[2:], jnp.bfloat16),
            pltpu.SemaphoreType.DMA((PARTS + 1,)),
        ],
        compiler_params=PARAMS,
        name="first",
    )(*in_hbm(right_cols.transpose(0, 3, 1, 2), right_blocks), packed)
    got_one = send(code_one, lambda r, c: (r, c ^ 1))
    across = send(packed, lambda r, c: ((r + 2) % n_row, c))
    near = send(packed, lambda r, c: (r ^ 1, c))
    own_cols = out_cols
    kept = pl.pallas_call(
        functools.partial(near_kernel, bs),
        out_shape=both,
        in_specs=[VMEM, VMEM],
        out_specs=VMEM,
        scratch_shapes=[left_scratch],
        compiler_params=PARAMS,
        name="near",
    )(dense, near)
    one_cols = send(own_cols, along(1, 1))
    far_cols = [send(own_cols, along(2, 3)), send(own_cols, along(3, 2))]
    far = send(across, lambda r, c: (r ^ 1, c))
    code_two = pl.pallas_call(
        functools.partial(second_kernel, bs),
        out_shape=code,
        in_specs=[VMEM] * 2,
        out_specs=VMEM,
        scratch_shapes=[left_scratch],
        compiler_params=PARAMS,
        name="second",
    )(dense, across)
    got_two = send(code_two, lambda r, c: (r, c ^ 1))
    kept = pl.pallas_call(
        functools.partial(far_kernel, bs),
        out_shape=both,
        in_specs=[VMEM, VMEM, HBM],
        out_specs=VMEM,
        scratch_shapes=[left_scratch],
        input_output_aliases={2: 0},
        compiler_params=PARAMS,
        name="far",
    )(dense, far, kept)

    def summed(odd, code, *held):
        scratch = [pltpu.VMEM((2 * wide_cols, rows, LANES), jnp.float32)]
        scratch += odd * [pltpu.VMEM(small.shape, small.dtype)]
        return pl.pallas_call(
            functools.partial(sum_kernel, bs, odd),
            out_shape=(2 + odd) * (small,),
            in_specs=[SMEM] * 3 + [VMEM] * (2 + odd),
            out_specs=(2 + odd) * (VMEM,),
            scratch_shapes=scratch,
            compiler_params=PARAMS,
            name="sum",
        )(own_cols, one_cols, far_cols[odd], kept, code, *held)

    a, held = summed(0, got_one)
    got = [send(a, along(2, 3))]
    a, b, own = summed(1, got_two, held)
    got += [send(a, along(3, 2)), send(b, along(1, 1)), own]
    return pl.pallas_call(
        functools.partial(last_kernel, bs),
        out_shape=jax.ShapeDtypeStruct((1, 1, ib, no, bs, bs), jnp.float32),
        in_specs=[VMEM] * len(got),
        out_specs=VMEM,
        compiler_params=PARAMS,
        name="last",
    )(*got)


def solution(mesh):
    in_specs = (
        P("row", "col", None, None, None, None),
        P("row", "col", None, None),
        P("row", "col", None, None, None, None),
        P("row", "col", None, None),
        P("row", "col", None, None),
    )
    out_specs = P("row", "col", None, None, None, None)
    n_row, n_col = mesh.shape["row"], mesh.shape["col"]
    body = functools.partial(grid_path, n_row, n_col) if (n_row, n_col) == (4, TICKS) else ring
    return jax.shard_map(body, mesh=mesh, in_specs=in_specs, out_specs=out_specs, check_vma=False)
```

```python
import functools

import jax
import jax.numpy as jnp
from jax import lax
from jax.experimental import pallas as pl
from jax.experimental.pallas import tpu as pltpu
from jax.sharding import PartitionSpec as P

TICKS = 8
LANES = 128
PAD = 16
TOP = 32767.0
GRAIN = 8192.0


def shifted(value, axis, steps):
    count = lax.axis_size(axis)
    pairs = [(source, (source + steps) % count) for source in range(count)]
    return lax.ppermute(value, axis, pairs)


def one_tick(left, left_cols, right, right_cols, pattern):
    inner = right.shape[0]
    pick_row = (left_cols[:, :, None] == jnp.arange(inner, dtype=jnp.int32)[None, None, :]).astype(
        jnp.float32
    )
    match = (right_cols[None, None, :, :] == pattern[:, :, None, None]).astype(jnp.float32)
    select = jnp.einsum("iak,iokb->iaokb", pick_row, match).astype(jnp.bfloat16)
    chosen = jnp.einsum(
        "iaokb,kbyz->iaoyz", select, right, preferred_element_type=jnp.float32
    ).astype(jnp.bfloat16)
    return jnp.einsum("iaxy,iaoyz->ioxz", left, chosen, preferred_element_type=jnp.float32)


def ring(left_blocks, left_cols, right_blocks, right_cols, out_cols):
    left = left_blocks[0, 0]
    left_index = left_cols[0, 0]
    right = right_blocks[0, 0]
    right_index = right_cols[0, 0]
    pattern = out_cols[0, 0]
    total = jnp.zeros((left.shape[0], pattern.shape[1], left.shape[2], left.shape[3]), jnp.float32)
    carried = shifted(pattern, "col", 1 - TICKS)
    for step in range(TICKS):
        total = total + one_tick(left, left_index, right, right_index, carried)
        if step + 1 < TICKS:
            total, carried = shifted((total, carried), "col", 1)
            left, left_index = shifted((left, left_index), "row", 1)
    return total[None, None]


def encode(parts, code_ref):
    rows = parts[0].shape[0]
    row = lax.broadcasted_iota(jnp.int32, (PAD, LANES), 0)
    scales = jnp.zeros((PAD, LANES), jnp.float32)
    for m, value in enumerate(parts):
        peak = jnp.maximum(jnp.max(jnp.abs(value), axis=0, keepdims=True), 2.0**-100)
        power = jnp.floor(jnp.log2(peak))
        shrink = jnp.exp2(-power)
        grains = jnp.ceil(peak * shrink * GRAIN) + 1.0
        factor = (TOP * GRAIN / grains) * shrink
        code_ref[m * rows : (m + 1) * rows] = jnp.round(value * factor).astype(jnp.int16)
        scales = jnp.where(row == m, power, jnp.where(row == PAD // 2 + m, grains, scales))
    code_ref[len(parts) * rows :] = scales.astype(jnp.int16)


def decoded(code_ref, rows):
    count = code_ref.shape[0] // rows
    tile = code_ref[count * rows :].astype(jnp.float32)
    scales = jnp.exp2(tile[: PAD // 2]) * (tile[PAD // 2 :] * (1.0 / (TOP * GRAIN)))
    for m in range(count):
        yield code_ref[m * rows : (m + 1) * rows].astype(jnp.float32) * scales[m : m + 1]


def spread_left(packed_ref, rows, half, dense_ref):
    side = lax.broadcasted_iota(jnp.int32, (1, LANES), 1) // half
    index = packed_ref[rows : rows + PAD, :].astype(jnp.float32)
    for i in range(rows // half):
        here, there, data, turned = [], [], [], []
        for b in range(packed_ref.shape[1] // LANES):
            lanes = slice(b * LANES, (b + 1) * LANES)
            column = index[i : i + 1, lanes].astype(jnp.int32)
            here.append(jnp.broadcast_to(column - side, (PAD, LANES)))
            there.append(jnp.broadcast_to(pltpu.roll(column, half, 1) - side, (PAD, LANES)))
            data.append(packed_ref[i * half : (i + 1) * half, lanes])
            turned.append(pltpu.roll(data[-1], half, 1))
        for m in range(dense_ref.shape[1] // LANES):
            masks = [(h == 2 * m, t == 2 * m) for h, t in zip(here, there)]
            for top in range(0, half, PAD):
                total = jnp.zeros((PAD, LANES), jnp.bfloat16)
                for b, (stays, turns) in enumerate(masks):
                    total = jnp.where(stays, data[b][top : top + PAD], total)
                    total = jnp.where(turns, turned[b][top : top + PAD], total)
                rows_of = slice(i * half + top, i * half + top + PAD)
                dense_ref[rows_of, m * LANES : (m + 1) * LANES] = total


def product(left, dense_ref):
    found = []
    for m in range(0, dense_ref.shape[0], 2):
        pair = jnp.concatenate([dense_ref[m], dense_ref[m + 1]], axis=1)
        part = jnp.dot(left, pair, preferred_element_type=jnp.float32)
        found += [part[:, :LANES], part[:, LANES:]]
    return found


def place(blocks, dense_ref):
    half = blocks[0][0].shape[0]
    side = lax.broadcasted_iota(jnp.int32, (half, LANES), 1) // half
    work = []
    for block, row, col in blocks:
        both = jnp.concatenate([block.astype(jnp.float32)]*2, axis=1).astype(jnp.bfloat16)
        at = (lax.shift_right_logical(col, 1), slice(row * half, (row + 1) * half))
        work.append((at, jnp.where(side == (col & 1), both, dense_ref[at])))
    for at, value in work:
        dense_ref[at] = value


def pack_kernel(cols_hbm, left_hbm, packed_ref, cols_ref, left_ref, sem):
    ib, nl, half, _ = left_ref.shape
    rows = ib * half
    copies = [
        pltpu.make_async_copy(cols_hbm, cols_ref, sem.at[0]),
        pltpu.make_async_copy(left_hbm.at[0, 0], left_ref, sem.at[1]),
    ]
    for copy in copies:
        copy.start()
    side = lax.broadcasted_iota(jnp.int32, (PAD, LANES), 1) // half
    row = lax.broadcasted_iota(jnp.int32, (PAD, LANES), 0)
    copies[0].wait()
    for b in range(nl // 2):
        index = jnp.zeros((PAD, LANES), jnp.int32)
        for i in range(ib):
            cols = jnp.where(side == 0, cols_ref[0, 0, i, 2 * b], cols_ref[0, 0, i, 2 * b + 1])
            index = jnp.where(row == i, cols, index)
        packed_ref[rows:, b * LANES : (b + 1) * LANES] = index.astype(jnp.float32).astype(jnp.bfloat16)
    copies[1].wait()
    for b in range(nl // 2):
        for i in range(ib):
            pair = jnp.concatenate([left_ref[i, 2 * b], left_ref[i, 2 * b + 1]], axis=1)
            packed_ref[i * half : (i + 1) * half, b * LANES : (b + 1) * LANES] = pair


def first_kernel(
    cols_hbm, right_hbm, packed_ref, dense_ref, code_ref, left_ref, cols_ref, right_ref, sem
):
    kb, kept, half, _ = right_ref.shape
    rows = left_ref.shape[0]
    parts = sem.shape[0] - 1
    step = kb // parts
    pairs = [(cols_hbm, cols_ref)]
    for part in range(parts):
        here = pl.ds(part * step, step)
        pairs.append((right_hbm.at[0, 0, here], right_ref.at[here]))
    copies = [pltpu.make_async_copy(*pair, sem.at[n]) for n, pair in enumerate(pairs)]
    for copy in copies:
        copy.start()
    dense_ref[...] = jnp.zeros_like(dense_ref)
    spread_left(packed_ref, rows, half, left_ref)
    copies[0].wait()
    for part in range(parts):
        copies[part + 1].wait()
        for e in range(kept):
            ks = range(part * step, (part + 1) * step)
            place([(right_ref[k, e], k, cols_ref[0, e, 0, k]) for k in ks], dense_ref)
    encode(product(left_ref[...], dense_ref), code_ref)


def second_kernel(half, dense_ref, packed_ref, code_ref, left_ref):
    spread_left(packed_ref, left_ref.shape[0], half, left_ref)
    encode(product(left_ref[...], dense_ref), code_ref)


def swapped():
    return (lax.axis_index("col") + lax.axis_index("row")) % 2


def near_kernel(half, dense_ref, packed_ref, kept_ref, left_ref):
    spread_left(packed_ref, left_ref.shape[0], half, left_ref)
    slot = swapped()
    for m, part in enumerate(product(left_ref[...], dense_ref)):
        kept_ref[slot, m] = part


def far_kernel(half, dense_ref, packed_ref, _, kept_ref, left_ref):
    spread_left(packed_ref, left_ref.shape[0], half, left_ref)
    slot = 1 - swapped()
    for m, part in enumerate(product(left_ref[...], dense_ref)):
        kept_ref[slot, m] = part


def sum_kernel(half, odd, own_ref, one_ref, far_ref, kept_ref, code_ref, *refs):
    if odd:
        held_ref, a_ref, b_ref, keep_ref, wide_ref, new_ref = refs
    else:
        a_ref, new_ref, wide_ref = refs
    _, pairs, rows, _ = kept_ref.shape
    for m, part in enumerate(decoded(code_ref, rows)):
        total = kept_ref[odd, m] + part
        wide_ref[m] = total
        wide_ref[pairs + m] = pltpu.roll(total, half, 1)
    low = lax.broadcasted_iota(jnp.int32, (half, LANES), 1) < half
    stays = (lax.axis_index("col") % 2) == odd

    def pick(near, i, o):
        picked = []
        for side in range(2):
            at = (0, 0, i, o + side)
            j = jnp.where(stays, own_ref[at], one_ref[at]) if near else far_ref[at]
            slot = lax.shift_right_logical(j, 1) + pairs * ((j + side) & 1)
            picked.append(wide_ref[slot, i * half : (i + 1) * half, :])
        return jnp.where(low, picked[0], picked[1])

    for near, target in ((False, a_ref), (True, new_ref)):
        steps = range(0, own_ref.shape[3], 2)
        encode([jnp.concatenate([pick(near, i, o) for i in range(rows // half)], axis=0) for o in steps], target)
    if odd:
        b_ref[...] = jnp.where(stays, held_ref[...], new_ref[...])
        keep_ref[...] = jnp.where(stays, new_ref[...], held_ref[...])


def last_kernel(half, a_ref, b_ref, c_ref, own_ref, out_ref):
    ib = out_ref.shape[2]
    arrived = [decoded(ref, ib * half) for ref in (a_ref, b_ref, c_ref, own_ref)]
    for m, (a, b, c, own) in enumerate(zip(*arrived)):
        total = (a + own) + (b + c)
        for i in range(ib):
            part = total[i * half : (i + 1) * half]
            out_ref[0, 0, i, 2 * m] = part[:, :half]
            out_ref[0, 0, i, 2 * m + 1] = part[:, half:]


VMEM = pl.BlockSpec(memory_space=pltpu.VMEM)
SMEM = pl.BlockSpec(memory_space=pltpu.SMEM)
HBM = pl.BlockSpec(memory_space=pltpu.HBM)
PARTS = 4
COST = pl.CostEstimate(flops=2000000000, bytes_accessed=20000000, transcendentals=0)
PARAMS = pltpu.CompilerParams(vmem_limit_bytes=40 * 2**20)


def grid_path(n_row, n_col, left_blocks, left_cols, right_blocks, right_cols, out_cols):
    _, _, ib, nl, bs, _ = left_blocks.shape
    kb = right_blocks.shape[2]
    jb = kb
    no = out_cols.shape[3]
    rows = ib * bs

    def send(value, to):
        pairs = []
        for r in range(n_row):
            for c in range(n_col):
                target = to(r, c)
                pairs.append((r * n_col + c, target[0] * n_col + target[1]))
        return lax.ppermute(value, ("row", "col"), pairs)

    def along(even, odd):
        return lambda r, c: (r, c ^ (2 * (odd if c % 2 else even)))

    wide_cols, no_cols = jb * bs // LANES, no * bs // LANES
    code = jax.ShapeDtypeStruct((wide_cols * rows + PAD, LANES), jnp.int16)
    small = jax.ShapeDtypeStruct((no_cols * rows + PAD, LANES), jnp.int16)
    both = jax.ShapeDtypeStruct((2, wide_cols, rows, LANES), jnp.float32)
    left_scratch = pltpu.VMEM((rows, kb * bs), jnp.bfloat16)
    def in_hbm(*arrays):
        return [pltpu.with_memory_space_constraint(array, pltpu.HBM) for array in arrays]

    packed = pl.pallas_call(
        pack_kernel,
        out_shape=jax.ShapeDtypeStruct((rows + PAD, nl * bs), jnp.bfloat16),
        in_specs=[HBM] * 2,
        out_specs=VMEM,
        scratch_shapes=[
            pltpu.SMEM(left_cols.shape[:2] + (ib, nl), jnp.int32),
            pltpu.VMEM(left_blocks.shape[2:], jnp.bfloat16),
            pltpu.SemaphoreType.DMA((2,)),
        ],
        compiler_params=PARAMS,
        name="pack",
    )(*in_hbm(left_cols, left_blocks))
    one_cols = send(out_cols, along(1, 1))
    dense, code_one = pl.pallas_call(
        first_kernel,
        out_shape=(
            jax.ShapeDtypeStruct((wide_cols, kb * bs, LANES), jnp.bfloat16),
            code,
        ),
        in_specs=[HBM, HBM, VMEM],
        out_specs=(VMEM, VMEM),
        scratch_shapes=[
            left_scratch,
            pltpu.SMEM((1, right_cols.shape[3], 1, kb), jnp.int32),
            pltpu.VMEM(right_blocks.shape[2:], jnp.bfloat16),
            pltpu.SemaphoreType.DMA((PARTS + 1,)),
        ],
        compiler_params=PARAMS,
        name="first",
    )(*in_hbm(right_cols.transpose(0, 3, 1, 2), right_blocks), packed)
    got_one = send(code_one, lambda r, c: (r, c ^ 1))
    across = send(packed, lambda r, c: ((r + 2) % n_row, c))
    dense, packed = lax.optimization_barrier((dense, packed))
    near = send(packed, lambda r, c: (r ^ 1, c))
    kept = pl.pallas_call(
        functools.partial(near_kernel, bs),
        out_shape=both,
        in_specs=[VMEM] * 2,
        out_specs=VMEM,
        scratch_shapes=[left_scratch],
        compiler_params=PARAMS,
        name="near",
    )(dense, near)
    far = send(across, lambda r, c: (r ^ 1, c))
    code_two = pl.pallas_call(
        functools.partial(second_kernel, bs),
        out_shape=code,
        in_specs=[VMEM] * 2,
        out_specs=VMEM,
        scratch_shapes=[left_scratch],
        compiler_params=PARAMS,
        name="second",
    )(dense, across)
    far_cols = (send(out_cols, along(2, 3)), send(out_cols, along(3, 2)))
    got_two = send(code_two, lambda r, c: (r, c ^ 1))
    kept = pl.pallas_call(
        functools.partial(far_kernel, bs),
        out_shape=both,
        in_specs=[VMEM, VMEM, HBM],
        out_specs=VMEM,
        scratch_shapes=[left_scratch],
        input_output_aliases={2: 0},
        compiler_params=PARAMS,
        name="far",
    )(dense, far, kept)

    def summed(odd, code, *held):
        scratch = [pltpu.VMEM((2 * wide_cols, rows, LANES), jnp.float32)]
        scratch += odd * [pltpu.VMEM(small.shape, small.dtype)]
        return pl.pallas_call(
            functools.partial(sum_kernel, bs, odd),
            out_shape=(2 + odd) * (small,),
            in_specs=[SMEM] * 3 + [VMEM] * (2 + odd),
            out_specs=(2 + odd) * (VMEM,),
            scratch_shapes=scratch,
            compiler_params=PARAMS,
            cost_estimate=None if odd else COST,
            name="sum",
        )(out_cols, one_cols, far_cols[odd], kept, code, *held)

    a, held = summed(0, got_one)
    got = [send(a, along(2, 3))]
    a, b, own = summed(1, got_two, held)
    got += [send(a, along(3, 2)), send(b, along(1, 1)), own]
    return pl.pallas_call(
        functools.partial(last_kernel, bs),
        out_shape=jax.ShapeDtypeStruct((1, 1, ib, no, bs, bs), jnp.float32),
        in_specs=[VMEM] * len(got),
        out_specs=VMEM,
        compiler_params=PARAMS,
        name="last",
    )(*got)


def solution(mesh):
    in_specs = (
        P("row", "col", None, None, None, None),
        P("row", "col", None, None),
        P("row", "col", None, None, None, None),
        P("row", "col", None, None),
        P("row", "col", None, None),
    )
    out_specs = P("row", "col", None, None, None, None)
    n_row, n_col = mesh.shape["row"], mesh.shape["col"]
    body = functools.partial(grid_path, n_row, n_col) if (n_row, n_col) == (4, TICKS) else ring
    return jax.shard_map(body, mesh=mesh, in_specs=in_specs, out_specs=out_specs, check_vma=False)
```

```python
import functools

import jax
import jax.numpy as jnp
from jax import lax
from jax.experimental import pallas as pl
from jax.experimental.pallas import tpu as pltpu
from jax.sharding import PartitionSpec as P

TICKS = 8
LANES = 128
PAD = 16
TOP = 32767.0
GRAIN = 8192.0


def shifted(value, axis, steps):
    count = lax.axis_size(axis)
    pairs = [(source, (source + steps) % count) for source in range(count)]
    return lax.ppermute(value, axis, pairs)


def one_tick(left, left_cols, right, right_cols, pattern):
    inner = right.shape[0]
    pick_row = (left_cols[:, :, None] == jnp.arange(inner, dtype=jnp.int32)[None, None, :]).astype(
        jnp.float32
    )
    match = (right_cols[None, None, :, :] == pattern[:, :, None, None]).astype(jnp.float32)
    select = jnp.einsum("iak,iokb->iaokb", pick_row, match).astype(jnp.bfloat16)
    chosen = jnp.einsum(
        "iaokb,kbyz->iaoyz", select, right, preferred_element_type=jnp.float32
    ).astype(jnp.bfloat16)
    return jnp.einsum("iaxy,iaoyz->ioxz", left, chosen, preferred_element_type=jnp.float32)


def ring(left_blocks, left_cols, right_blocks, right_cols, out_cols):
    left = left_blocks[0, 0]
    left_index = left_cols[0, 0]
    right = right_blocks[0, 0]
    right_index = right_cols[0, 0]
    pattern = out_cols[0, 0]
    total = jnp.zeros((left.shape[0], pattern.shape[1], left.shape[2], left.shape[3]), jnp.float32)
    carried = shifted(pattern, "col", 1 - TICKS)
    for step in range(TICKS):
        total = total + one_tick(left, left_index, right, right_index, carried)
        if step + 1 < TICKS:
            total, carried = shifted((total, carried), "col", 1)
            left, left_index = shifted((left, left_index), "row", 1)
    return total[None, None]


def encode(parts, code_ref):
    rows = parts[0].shape[0]
    row = lax.broadcasted_iota(jnp.int32, (PAD, LANES), 0)
    scales = jnp.zeros((PAD, LANES), jnp.float32)
    for m, value in enumerate(parts):
        peak = jnp.maximum(jnp.max(jnp.abs(value), axis=0, keepdims=True), 2.0**-100)
        power = jnp.floor(jnp.log2(peak))
        shrink = jnp.exp2(-power)
        grains = jnp.ceil(peak * shrink * GRAIN) + 1.0
        factor = (TOP * GRAIN / grains) * shrink
        code_ref[m * rows : (m + 1) * rows] = jnp.round(value * factor).astype(jnp.int16)
        scales = jnp.where(row == m, power, jnp.where(row == PAD // 2 + m, grains, scales))
    code_ref[len(parts) * rows :] = scales.astype(jnp.int16)


def decoded(code_ref, rows):
    count = code_ref.shape[0] // rows
    tile = code_ref[count * rows :].astype(jnp.float32)
    scales = jnp.exp2(tile[: PAD // 2]) * (tile[PAD // 2 :] * (1.0 / (TOP * GRAIN)))
    for m in range(count):
        yield code_ref[m * rows : (m + 1) * rows].astype(jnp.float32) * scales[m : m + 1]


def spread_left(packed_ref, rows, half, dense_ref):
    side = lax.broadcasted_iota(jnp.int32, (1, LANES), 1) // half
    count = packed_ref.shape[0] // rows
    index = packed_ref[count * rows :].astype(jnp.float32)
    for i in range(rows // half):
        here, there, data, turned = [], [], [], []
        for b in range(count):
            column = index[i * count + b : i * count + b + 1].astype(jnp.int32)
            here.append(jnp.broadcast_to(column - side, (PAD, LANES)))
            there.append(jnp.broadcast_to(pltpu.roll(column, half, 1) - side, (PAD, LANES)))
            data.append(packed_ref[b * rows + i * half : b * rows + (i + 1) * half])
            turned.append(pltpu.roll(data[-1], half, 1))
        for m in range(dense_ref.shape[1] // LANES):
            masks = [(h == 2 * m, t == 2 * m) for h, t in zip(here, there)]
            for top in range(0, half, PAD):
                total = jnp.zeros((PAD, LANES), jnp.bfloat16)
                for b, (stays, turns) in enumerate(masks):
                    total = jnp.where(stays, data[b][top : top + PAD], total)
                    total = jnp.where(turns, turned[b][top : top + PAD], total)
                rows_of = slice(i * half + top, i * half + top + PAD)
                dense_ref[rows_of, m * LANES : (m + 1) * LANES] = total


def product(left, dense_ref):
    found = []
    for m in range(0, dense_ref.shape[0], 2):
        pair = jnp.concatenate([dense_ref[m], dense_ref[m + 1]], axis=1)
        part = jnp.dot(left, pair, preferred_element_type=jnp.float32)
        found += [part[:, :LANES], part[:, LANES:]]
    return found


def place(blocks, dense_ref):
    half = blocks[0][0].shape[0]
    side = lax.broadcasted_iota(jnp.int32, (half, LANES), 1) // half
    work = []
    for block, row, col in blocks:
        both = jnp.concatenate([block.astype(jnp.float32)]*2, axis=1).astype(jnp.bfloat16)
        at = (lax.shift_right_logical(col, 1), slice(row * half, (row + 1) * half))
        work.append((at, jnp.where(side == (col & 1), both, dense_ref[at])))
    for at, value in work:
        dense_ref[at] = value


def pack_kernel(cols_hbm, left_hbm, packed_ref, cols_ref, left_ref, sem):
    ib, nl, half, _ = left_ref.shape
    rows, count = ib * half, nl // 2
    copies = [pltpu.make_async_copy(cols_hbm, cols_ref, sem.at[ib])]
    for i in range(ib):
        copies.append(pltpu.make_async_copy(left_hbm.at[0, 0, i], left_ref.at[i], sem.at[i]))
    for copy in copies:
        copy.start()
    side = lax.broadcasted_iota(jnp.int32, (PAD, LANES), 1) // half
    row = lax.broadcasted_iota(jnp.int32, (PAD, LANES), 0)
    index = jnp.zeros((PAD, LANES), jnp.int32)
    copies[0].wait()
    for i in range(ib):
        for b in range(count):
            cols = jnp.where(side == 0, cols_ref[0, 0, i, 2 * b], cols_ref[0, 0, i, 2 * b + 1])
            index = jnp.where(row == i * count + b, cols, index)
    packed_ref[count * rows :] = index.astype(jnp.float32).astype(jnp.bfloat16)
    for i in range(ib):
        copies[1 + i].wait()
        for b in range(count):
            pair = jnp.concatenate([left_ref[i, 2 * b], left_ref[i, 2 * b + 1]], axis=1)
            packed_ref[b * rows + i * half : b * rows + (i + 1) * half] = pair


def first_kernel(
    cols_hbm, right_hbm, packed_ref, dense_ref, code_ref, left_ref, cols_ref, right_ref, sem
):
    kb, kept, half, _ = right_ref.shape
    rows = left_ref.shape[0]
    parts = sem.shape[0] - 1
    step = kb // parts
    pairs = [(cols_hbm, cols_ref)]
    for part in range(parts):
        here = pl.ds(part * step, step)
        pairs.append((right_hbm.at[0, 0, here], right_ref.at[here]))
    copies = [pltpu.make_async_copy(*pair, sem.at[n]) for n, pair in enumerate(pairs)]
    for copy in copies:
        copy.start()
    dense_ref[...] = jnp.zeros_like(dense_ref)
    spread_left(packed_ref, rows, half, left_ref)
    copies[0].wait()
    for part in range(parts):
        copies[part + 1].wait()
        for e in range(kept):
            ks = range(part * step, (part + 1) * step)
            place([(right_ref[k, e], k, cols_ref[0, e, 0, k]) for k in ks], dense_ref)
    encode(product(left_ref[...], dense_ref), code_ref)


def second_kernel(half, dense_ref, packed_ref, code_ref, left_ref):
    spread_left(packed_ref, left_ref.shape[0], half, left_ref)
    encode(product(left_ref[...], dense_ref), code_ref)


def swapped():
    return (lax.axis_index("col") + lax.axis_index("row")) % 2


def kept_kernel(half, dense_ref, near_ref, far_ref, kept_ref, left_ref):
    _, _, rows, _ = kept_ref.shape
    spread_left(near_ref, rows, half, left_ref.at[:rows])
    spread_left(far_ref, rows, half, left_ref.at[rows:])
    slot = swapped()
    for m, part in enumerate(product(left_ref[...], dense_ref)):
        kept_ref[slot, m] = part[:rows]
        kept_ref[1 - slot, m] = part[rows:]


def sum_kernel(half, odd, own_ref, one_ref, far_ref, kept_ref, code_ref, *refs):
    if odd:
        held_ref, a_ref, b_ref, keep_ref, wide_ref, new_ref = refs
    else:
        a_ref, new_ref, wide_ref = refs
    _, pairs, rows, _ = kept_ref.shape
    for m, part in enumerate(decoded(code_ref, rows)):
        total = kept_ref[odd, m] + part
        wide_ref[m] = total
        wide_ref[pairs + m] = pltpu.roll(total, half, 1)
    low = lax.broadcasted_iota(jnp.int32, (half, LANES), 1) < half
    stays = (lax.axis_index("col") % 2) == odd

    def pick(near, i, o):
        picked = []
        for side in range(2):
            at = (0, 0, i, o + side)
            j = jnp.where(stays, own_ref[at], one_ref[at]) if near else far_ref[at]
            slot = lax.shift_right_logical(j, 1) + pairs * ((j + side) & 1)
            picked.append(wide_ref[slot, i * half : (i + 1) * half, :])
        return jnp.where(low, picked[0], picked[1])

    for near, target in ((False, a_ref), (True, new_ref)):
        steps = range(0, own_ref.shape[3], 2)
        encode([jnp.concatenate([pick(near, i, o) for i in range(rows // half)], axis=0) for o in steps], target)
    if odd:
        b_ref[...] = jnp.where(stays, held_ref[...], new_ref[...])
        keep_ref[...] = jnp.where(stays, new_ref[...], held_ref[...])


def last_kernel(half, a_ref, b_ref, c_ref, own_ref, out_ref):
    ib = out_ref.shape[2]
    arrived = [decoded(ref, ib * half) for ref in (a_ref, b_ref, c_ref, own_ref)]
    for m, (a, b, c, own) in enumerate(zip(*arrived)):
        total = (a + own) + (b + c)
        for i in range(ib):
            part = total[i * half : (i + 1) * half]
            out_ref[0, 0, i, 2 * m] = part[:, :half]
            out_ref[0, 0, i, 2 * m + 1] = part[:, half:]


VMEM = pl.BlockSpec(memory_space=pltpu.VMEM)
SMEM = pl.BlockSpec(memory_space=pltpu.SMEM)
HBM = pl.BlockSpec(memory_space=pltpu.HBM)
PARTS = 4
COST = pl.CostEstimate(flops=2000000000, bytes_accessed=20000000, transcendentals=0)
PARAMS = pltpu.CompilerParams(vmem_limit_bytes=40 * 2**20)


def grid_path(n_row, n_col, left_blocks, left_cols, right_blocks, right_cols, out_cols):
    _, _, ib, nl, bs, _ = left_blocks.shape
    kb = right_blocks.shape[2]
    jb = kb
    no = out_cols.shape[3]
    rows = ib * bs

    def send(value, to):
        pairs = []
        for r in range(n_row):
            for c in range(n_col):
                target = to(r, c)
                pairs.append((r * n_col + c, target[0] * n_col + target[1]))
        return lax.ppermute(value, ("row", "col"), pairs)

    def along(even, odd):
        return lambda r, c: (r, c ^ (2 * (odd if c % 2 else even)))

    wide_cols, no_cols = jb * bs // LANES, no * bs // LANES
    code = jax.ShapeDtypeStruct((wide_cols * rows + PAD, LANES), jnp.int16)
    small = jax.ShapeDtypeStruct((no_cols * rows + PAD, LANES), jnp.int16)
    both = jax.ShapeDtypeStruct((2, wide_cols, rows, LANES), jnp.float32)
    left_scratch = pltpu.VMEM((rows, kb * bs), jnp.bfloat16)
    def in_hbm(*arrays):
        return [pltpu.with_memory_space_constraint(array, pltpu.HBM) for array in arrays]

    packed = pl.pallas_call(
        pack_kernel,
        out_shape=jax.ShapeDtypeStruct((nl * bs // LANES * rows + PAD, LANES), jnp.bfloat16),
        in_specs=[HBM] * 2,
        out_specs=VMEM,
        scratch_shapes=[
            pltpu.SMEM(left_cols.shape[:2] + (ib, nl), jnp.int32),
            pltpu.VMEM(left_blocks.shape[2:], jnp.bfloat16),
            pltpu.SemaphoreType.DMA((ib + 1,)),
        ],
        compiler_params=PARAMS,
        name="pack",
    )(*in_hbm(left_cols, left_blocks))
    one_cols = send(out_cols, along(1, 1))
    dense, code_one = pl.pallas_call(
        first_kernel,
        out_shape=(
            jax.ShapeDtypeStruct((wide_cols, kb * bs, LANES), jnp.bfloat16),
            code,
        ),
        in_specs=[HBM, HBM, VMEM],
        out_specs=(VMEM, VMEM),
        scratch_shapes=[
            left_scratch,
            pltpu.SMEM((1, right_cols.shape[3], 1, kb), jnp.int32),
            pltpu.VMEM(right_blocks.shape[2:], jnp.bfloat16),
            pltpu.SemaphoreType.DMA((PARTS + 1,)),
        ],
        compiler_params=PARAMS,
        name="first",
    )(*in_hbm(right_cols.transpose(0, 3, 1, 2), right_blocks), packed)
    got_one = send(code_one, lambda r, c: (r, c ^ 1))
    across = send(packed, lambda r, c: ((r + 2) % n_row, c))
    dense, packed = lax.optimization_barrier((dense, packed))
    near = send(packed, lambda r, c: (r ^ 1, c))
    far = send(across, lambda r, c: (r ^ 1, c))
    code_two = pl.pallas_call(
        functools.partial(second_kernel, bs),
        out_shape=code,
        in_specs=[VMEM] * 2,
        out_specs=VMEM,
        scratch_shapes=[left_scratch],
        compiler_params=PARAMS,
        name="second",
    )(dense, across)
    far_cols = (send(out_cols, along(2, 3)), send(out_cols, along(3, 2)))
    got_two = send(code_two, lambda r, c: (r, c ^ 1))
    kept = pl.pallas_call(
        functools.partial(kept_kernel, bs),
        out_shape=both,
        in_specs=[VMEM] * 3,
        out_specs=VMEM,
        scratch_shapes=[pltpu.VMEM((2 * rows, kb * bs), jnp.bfloat16)],
        compiler_params=PARAMS,
        name="kept",
    )(dense, near, far)

    def summed(odd, code, *held):
        scratch = [pltpu.VMEM((2 * wide_cols, rows, LANES), jnp.float32)]
        scratch += odd * [pltpu.VMEM(small.shape, small.dtype)]
        return pl.pallas_call(
            functools.partial(sum_kernel, bs, odd),
            out_shape=(2 + odd) * (small,),
            in_specs=[SMEM] * 3 + [VMEM] * (2 + odd),
            out_specs=(2 + odd) * (VMEM,),
            scratch_shapes=scratch,
            compiler_params=PARAMS,
            cost_estimate=None if odd else COST,
            name="sum",
        )(out_cols, one_cols, far_cols[odd], kept, code, *held)

    a, held = summed(0, got_one)
    got = [send(a, along(2, 3))]
    a, b, own = summed(1, got_two, held)
    got += [send(a, along(3, 2)), send(b, along(1, 1)), own]
    return pl.pallas_call(
        functools.partial(last_kernel, bs),
        out_shape=jax.ShapeDtypeStruct((1, 1, ib, no, bs, bs), jnp.float32),
        in_specs=[VMEM] * len(got),
        out_specs=VMEM,
        compiler_params=PARAMS,
        name="last",
    )(*got)


def solution(mesh):
    in_specs = (
        P("row", "col", None, None, None, None),
        P("row", "col", None, None),
        P("row", "col", None, None, None, None),
        P("row", "col", None, None),
        P("row", "col", None, None),
    )
    out_specs = P("row", "col", None, None, None, None)
    n_row, n_col = mesh.shape["row"], mesh.shape["col"]
    body = functools.partial(grid_path, n_row, n_col) if (n_row, n_col) == (4, TICKS) else ring
    return jax.shard_map(body, mesh=mesh, in_specs=in_specs, out_specs=out_specs, check_vma=False)
```

```python
import functools

import jax
import jax.numpy as jnp
from jax import lax
from jax.experimental import pallas as pl
from jax.experimental.pallas import tpu as pltpu
from jax.sharding import PartitionSpec as P

TICKS = 8
LANES = 128
PAD = 16
TOP = 32767.0
GRAIN = 8192.0


def shifted(value, axis, steps):
    count = lax.axis_size(axis)
    pairs = [(source, (source + steps) % count) for source in range(count)]
    return lax.ppermute(value, axis, pairs)


def one_tick(left, left_cols, right, right_cols, pattern):
    inner = right.shape[0]
    pick_row = (left_cols[:, :, None] == jnp.arange(inner, dtype=jnp.int32)[None, None, :]).astype(
        jnp.float32
    )
    match = (right_cols[None, None, :, :] == pattern[:, :, None, None]).astype(jnp.float32)
    select = jnp.einsum("iak,iokb->iaokb", pick_row, match).astype(jnp.bfloat16)
    chosen = jnp.einsum(
        "iaokb,kbyz->iaoyz", select, right, preferred_element_type=jnp.float32
    ).astype(jnp.bfloat16)
    return jnp.einsum("iaxy,iaoyz->ioxz", left, chosen, preferred_element_type=jnp.float32)


def ring(left_blocks, left_cols, right_blocks, right_cols, out_cols):
    left = left_blocks[0, 0]
    left_index = left_cols[0, 0]
    right = right_blocks[0, 0]
    right_index = right_cols[0, 0]
    pattern = out_cols[0, 0]
    total = jnp.zeros((left.shape[0], pattern.shape[1], left.shape[2], left.shape[3]), jnp.float32)
    carried = shifted(pattern, "col", 1 - TICKS)
    for step in range(TICKS):
        total = total + one_tick(left, left_index, right, right_index, carried)
        if step + 1 < TICKS:
            total, carried = shifted((total, carried), "col", 1)
            left, left_index = shifted((left, left_index), "row", 1)
    return total[None, None]


def encode(parts, code_ref):
    rows = parts[0].shape[0]
    row = lax.broadcasted_iota(jnp.int32, (PAD, LANES), 0)
    scales = jnp.zeros((PAD, LANES), jnp.float32)
    for m, value in enumerate(parts):
        peak = jnp.maximum(jnp.max(jnp.abs(value), axis=0, keepdims=True), 2.0**-100)
        power = jnp.floor(jnp.log2(peak))
        shrink = jnp.exp2(-power)
        grains = jnp.ceil(peak * shrink * GRAIN) + 1.0
        factor = (TOP * GRAIN / grains) * shrink
        code_ref[m * rows : (m + 1) * rows] = jnp.round(value * factor).astype(jnp.int32).astype(jnp.int16)
        scales = jnp.where(row == m, power, jnp.where(row == PAD // 2 + m, grains, scales))
    code_ref[len(parts) * rows :] = scales.astype(jnp.int16)


def decoded(code_ref, rows):
    count = code_ref.shape[0] // rows
    tile = code_ref[count * rows :].astype(jnp.float32)
    scales = jnp.exp2(tile[: PAD // 2]) * (tile[PAD // 2 :] * (1.0 / (TOP * GRAIN)))
    for m in range(count):
        yield code_ref[m * rows : (m + 1) * rows].astype(jnp.float32) * scales[m : m + 1]


def spread_left(packed_ref, rows, half, dense_ref):
    side = lax.broadcasted_iota(jnp.int32, (1, LANES), 1) // half
    count = packed_ref.shape[0] // rows
    index = packed_ref[count * rows :].astype(jnp.float32)
    for i in range(rows // half):
        here, there, data, turned = [], [], [], []
        for b in range(count):
            column = index[i * count + b : i * count + b + 1].astype(jnp.int32)
            here.append(jnp.broadcast_to(column - side, (PAD, LANES)))
            there.append(jnp.broadcast_to(pltpu.roll(column, half, 1) - side, (PAD, LANES)))
            data.append(packed_ref[b * rows + i * half : b * rows + (i + 1) * half])
            turned.append(pltpu.roll(data[-1], half, 1))
        for m in range(dense_ref.shape[1] // LANES):
            masks = [(h == 2 * m, t == 2 * m) for h, t in zip(here, there)]
            for top in range(0, half, PAD):
                total = jnp.zeros((PAD, LANES), jnp.bfloat16)
                for b, (stays, turns) in enumerate(masks):
                    total = jnp.where(stays, data[b][top : top + PAD], total)
                    total = jnp.where(turns, turned[b][top : top + PAD], total)
                rows_of = slice(i * half + top, i * half + top + PAD)
                dense_ref[rows_of, m * LANES : (m + 1) * LANES] = total


def product(left, dense_ref):
    found = []
    for m in range(0, dense_ref.shape[0], 2):
        pair = jnp.concatenate([dense_ref[m], dense_ref[m + 1]], axis=1)
        part = jnp.dot(left, pair, preferred_element_type=jnp.float32)
        found += [part[:, :LANES], part[:, LANES:]]
    return found


def place(blocks, dense_ref):
    half = blocks[0][0].shape[0]
    side = lax.broadcasted_iota(jnp.int32, (half, LANES), 1) // half
    work = []
    for block, row, col in blocks:
        both = jnp.concatenate([block.astype(jnp.float32)]*2, axis=1).astype(jnp.bfloat16)
        at = (lax.shift_right_logical(col, 1), slice(row * half, (row + 1) * half))
        work.append((at, jnp.where(side == (col & 1), both, dense_ref[at])))
    for at, value in work:
        dense_ref[at] = value


def pack_kernel(cols_hbm, left_hbm, packed_ref, cols_ref, left_ref, sem):
    ib, nl, half, _ = left_ref.shape
    rows, count = ib * half, nl // 2
    copies = [pltpu.make_async_copy(cols_hbm, cols_ref, sem.at[ib])]
    for i in range(ib):
        copies.append(pltpu.make_async_copy(left_hbm.at[0, 0, i], left_ref.at[i], sem.at[i]))
    for copy in copies:
        copy.start()
    side = lax.broadcasted_iota(jnp.int32, (PAD, LANES), 1) // half
    row = lax.broadcasted_iota(jnp.int32, (PAD, LANES), 0)
    index = jnp.zeros((PAD, LANES), jnp.int32)
    copies[0].wait()
    for i in range(ib):
        for b in range(count):
            cols = jnp.where(side == 0, cols_ref[0, 0, i, 2 * b], cols_ref[0, 0, i, 2 * b + 1])
            index = jnp.where(row == i * count + b, cols, index)
    packed_ref[count * rows :] = index.astype(jnp.float32).astype(jnp.bfloat16)
    for i in range(ib):
        copies[1 + i].wait()
        for b in range(count):
            pair = jnp.concatenate([left_ref[i, 2 * b], left_ref[i, 2 * b + 1]], axis=1)
            packed_ref[b * rows + i * half : b * rows + (i + 1) * half] = pair


def first_kernel(
    cols_hbm, right_hbm, packed_ref, dense_ref, code_ref, left_ref, cols_ref, right_ref, sem
):
    kb, kept, half, _ = right_ref.shape
    rows = left_ref.shape[0]
    parts = sem.shape[0] - 1
    step = kb // parts
    pairs = [(cols_hbm, cols_ref)]
    for part in range(parts):
        here = pl.ds(part * step, step)
        pairs.append((right_hbm.at[0, 0, here], right_ref.at[here]))
    copies = [pltpu.make_async_copy(*pair, sem.at[n]) for n, pair in enumerate(pairs)]
    for copy in copies:
        copy.start()
    dense_ref[...] = jnp.zeros_like(dense_ref)
    spread_left(packed_ref, rows, half, left_ref)
    copies[0].wait()
    for part in range(parts):
        copies[part + 1].wait()
        for e in range(kept):
            ks = range(part * step, (part + 1) * step)
            place([(right_ref[k, e], k, cols_ref[0, e, 0, k]) for k in ks], dense_ref)
    encode(product(left_ref[...], dense_ref), code_ref)


def second_kernel(half, dense_ref, packed_ref, code_ref, left_ref):
    spread_left(packed_ref, left_ref.shape[0], half, left_ref)
    encode(product(left_ref[...], dense_ref), code_ref)


def swapped():
    return (lax.axis_index("col") + lax.axis_index("row")) % 2


def kept_kernel(half, dense_ref, near_ref, far_ref, kept_ref, left_ref):
    _, _, rows, _ = kept_ref.shape
    spread_left(near_ref, rows, half, left_ref.at[:rows])
    spread_left(far_ref, rows, half, left_ref.at[rows:])
    slot = swapped()
    for m, part in enumerate(product(left_ref[...], dense_ref)):
        kept_ref[slot, m] = part[:rows]
        kept_ref[1 - slot, m] = part[rows:]


def sum_kernel(half, odd, own_ref, one_ref, far_ref, kept_ref, code_ref, *refs):
    if odd:
        held_ref, a_ref, b_ref, keep_ref, wide_ref, new_ref = refs
    else:
        a_ref, new_ref, wide_ref = refs
    _, pairs, rows, _ = kept_ref.shape
    for m, part in enumerate(decoded(code_ref, rows)):
        total = kept_ref[odd, m] + part
        wide_ref[m] = total
        wide_ref[pairs + m] = pltpu.roll(total, half, 1)
    low = lax.broadcasted_iota(jnp.int32, (half, LANES), 1) < half
    stays = (lax.axis_index("col") % 2) == odd

    def pick(near, i, o):
        picked = []
        for side in range(2):
            at = (0, 0, i, o + side)
            j = jnp.where(stays, own_ref[at], one_ref[at]) if near else far_ref[at]
            slot = lax.shift_right_logical(j, 1) + pairs * ((j + side) & 1)
            picked.append(wide_ref[slot, i * half : (i + 1) * half, :])
        return jnp.where(low, picked[0], picked[1])

    for near, target in ((False, a_ref), (True, new_ref)):
        steps = range(0, own_ref.shape[3], 2)
        encode([jnp.concatenate([pick(near, i, o) for i in range(rows // half)], axis=0) for o in steps], target)
    if odd:
        b_ref[...] = jnp.where(stays, held_ref[...], new_ref[...])
        keep_ref[...] = jnp.where(stays, new_ref[...], held_ref[...])


def last_kernel(half, a_ref, b_ref, c_ref, own_ref, out_hbm, out_ref, sem):
    ib = out_ref.shape[0]
    arrived = [decoded(ref, ib * half) for ref in (a_ref, b_ref, c_ref, own_ref)]
    copies = []
    for m, (a, b, c, own) in enumerate(zip(*arrived)):
        total = (a + own) + (b + c)
        for i in range(ib):
            part = total[i * half : (i + 1) * half]
            out_ref[i, 2 * m] = part[:, :half]
            out_ref[i, 2 * m + 1] = part[:, half:]
            here = pl.ds(2 * m, 2)
            copies.append(pltpu.make_async_copy(out_ref.at[i, here], out_hbm.at[0, 0, i, here], sem.at[m * ib + i]))
            copies[-1].start()
    for copy in copies:
        copy.wait()


VMEM = pl.BlockSpec(memory_space=pltpu.VMEM)
SMEM = pl.BlockSpec(memory_space=pltpu.SMEM)
HBM = pl.BlockSpec(memory_space=pltpu.HBM)
PARTS = 4
COST = pl.CostEstimate(flops=2000000000, bytes_accessed=20000000, transcendentals=0)
PARAMS = pltpu.CompilerParams(vmem_limit_bytes=40 * 2**20)


def grid_path(n_row, n_col, left_blocks, left_cols, right_blocks, right_cols, out_cols):
    _, _, ib, nl, bs, _ = left_blocks.shape
    kb = right_blocks.shape[2]
    jb = kb
    no = out_cols.shape[3]
    rows = ib * bs

    def send(value, to):
        pairs = []
        for r in range(n_row):
            for c in range(n_col):
                target = to(r, c)
                pairs.append((r * n_col + c, target[0] * n_col + target[1]))
        return lax.ppermute(value, ("row", "col"), pairs)

    def along(even, odd):
        return lambda r, c: (r, c ^ (2 * (odd if c % 2 else even)))

    wide_cols, no_cols = jb * bs // LANES, no * bs // LANES
    code = jax.ShapeDtypeStruct((wide_cols * rows + PAD, LANES), jnp.int16)
    small = jax.ShapeDtypeStruct((no_cols * rows + PAD, LANES), jnp.int16)
    both = jax.ShapeDtypeStruct((2, wide_cols, rows, LANES), jnp.float32)
    left_scratch = pltpu.VMEM((rows, kb * bs), jnp.bfloat16)
    def in_hbm(*arrays):
        return [pltpu.with_memory_space_constraint(array, pltpu.HBM) for array in arrays]

    packed = pl.pallas_call(
        pack_kernel,
        out_shape=jax.ShapeDtypeStruct((nl * bs // LANES * rows + PAD, LANES), jnp.bfloat16),
        in_specs=[HBM] * 2,
        out_specs=VMEM,
        scratch_shapes=[
            pltpu.SMEM(left_cols.shape[:2] + (ib, nl), jnp.int32),
            pltpu.VMEM(left_blocks.shape[2:], jnp.bfloat16),
            pltpu.SemaphoreType.DMA((ib + 1,)),
        ],
        compiler_params=PARAMS,
        name="pack",
    )(*in_hbm(left_cols, left_blocks))
    one_cols = send(out_cols, along(1, 1))
    dense, code_one = pl.pallas_call(
        first_kernel,
        out_shape=(
            jax.ShapeDtypeStruct((wide_cols, kb * bs, LANES), jnp.bfloat16),
            code,
        ),
        in_specs=[HBM, HBM, VMEM],
        out_specs=(VMEM, VMEM),
        scratch_shapes=[
            left_scratch,
            pltpu.SMEM((1, right_cols.shape[3], 1, kb), jnp.int32),
            pltpu.VMEM(right_blocks.shape[2:], jnp.bfloat16),
            pltpu.SemaphoreType.DMA((PARTS + 1,)),
        ],
        compiler_params=PARAMS,
        name="first",
    )(*in_hbm(right_cols.transpose(0, 3, 1, 2), right_blocks), packed)
    got_one = send(code_one, lambda r, c: (r, c ^ 1))
    across = send(packed, lambda r, c: ((r + 2) % n_row, c))
    dense, packed = lax.optimization_barrier((dense, packed))
    near = send(packed, lambda r, c: (r ^ 1, c))
    far = send(across, lambda r, c: (r ^ 1, c))
    code_two = pl.pallas_call(
        functools.partial(second_kernel, bs),
        out_shape=code,
        in_specs=[VMEM] * 2,
        out_specs=VMEM,
        scratch_shapes=[left_scratch],
        compiler_params=PARAMS,
        name="second",
    )(dense, across)
    far_cols = (send(out_cols, along(2, 3)), send(out_cols, along(3, 2)))
    got_two = send(code_two, lambda r, c: (r, c ^ 1))
    kept = pl.pallas_call(
        functools.partial(kept_kernel, bs),
        out_shape=both,
        in_specs=[VMEM] * 3,
        out_specs=VMEM,
        scratch_shapes=[pltpu.VMEM((2 * rows, kb * bs), jnp.bfloat16)],
        compiler_params=PARAMS,
        name="kept",
    )(dense, near, far)

    def summed(odd, code, *held):
        scratch = [pltpu.VMEM((2 * wide_cols, rows, LANES), jnp.float32)]
        scratch += odd * [pltpu.VMEM(small.shape, small.dtype)]
        return pl.pallas_call(
            functools.partial(sum_kernel, bs, odd),
            out_shape=(2 + odd) * (small,),
            in_specs=[SMEM] * 3 + [VMEM] * (2 + odd),
            out_specs=(2 + odd) * (VMEM,),
            scratch_shapes=scratch,
            compiler_params=PARAMS,
            cost_estimate=None if odd else COST,
            name="sum",
        )(out_cols, one_cols, far_cols[odd], kept, code, *held)

    a, held = summed(0, got_one)
    got = [send(a, along(2, 3))]
    a, b, own = summed(1, got_two, held)
    got += [send(a, along(3, 2)), send(b, along(1, 1)), own]
    return pl.pallas_call(
        functools.partial(last_kernel, bs),
        out_shape=jax.ShapeDtypeStruct((1, 1, ib, no, bs, bs), jnp.float32),
        in_specs=[VMEM] * len(got),
        out_specs=HBM,
        scratch_shapes=[
            pltpu.VMEM((ib, no, bs, bs), jnp.float32),
            pltpu.SemaphoreType.DMA((ib * no // 2,)),
        ],
        compiler_params=PARAMS,
        name="last",
    )(*got)


def solution(mesh):
    in_specs = (
        P("row", "col", None, None, None, None),
        P("row", "col", None, None),
        P("row", "col", None, None, None, None),
        P("row", "col", None, None),
        P("row", "col", None, None),
    )
    out_specs = P("row", "col", None, None, None, None)
    n_row, n_col = mesh.shape["row"], mesh.shape["col"]
    body = functools.partial(grid_path, n_row, n_col) if (n_row, n_col) == (4, TICKS) else ring
    return jax.shard_map(body, mesh=mesh, in_specs=in_specs, out_specs=out_specs, check_vma=False)
```

```python
import functools

import jax
import jax.numpy as jnp
from jax import lax
from jax.experimental import pallas as pl
from jax.experimental.pallas import tpu as pltpu
from jax.sharding import PartitionSpec as P

TICKS = 8
LANES = 128
PAD = 16
TOP = 32767.0
GRAIN = 8192.0


def shifted(value, axis, steps):
    count = lax.axis_size(axis)
    pairs = [(source, (source + steps) % count) for source in range(count)]
    return lax.ppermute(value, axis, pairs)


def one_tick(left, left_cols, right, right_cols, pattern):
    inner = right.shape[0]
    pick_row = (left_cols[:, :, None] == jnp.arange(inner, dtype=jnp.int32)[None, None, :]).astype(
        jnp.float32
    )
    match = (right_cols[None, None, :, :] == pattern[:, :, None, None]).astype(jnp.float32)
    select = jnp.einsum("iak,iokb->iaokb", pick_row, match).astype(jnp.bfloat16)
    chosen = jnp.einsum(
        "iaokb,kbyz->iaoyz", select, right, preferred_element_type=jnp.float32
    ).astype(jnp.bfloat16)
    return jnp.einsum("iaxy,iaoyz->ioxz", left, chosen, preferred_element_type=jnp.float32)


def ring(left_blocks, left_cols, right_blocks, right_cols, out_cols):
    left = left_blocks[0, 0]
    left_index = left_cols[0, 0]
    right = right_blocks[0, 0]
    right_index = right_cols[0, 0]
    pattern = out_cols[0, 0]
    total = jnp.zeros((left.shape[0], pattern.shape[1], left.shape[2], left.shape[3]), jnp.float32)
    carried = shifted(pattern, "col", 1 - TICKS)
    for step in range(TICKS):
        total = total + one_tick(left, left_index, right, right_index, carried)
        if step + 1 < TICKS:
            total, carried = shifted((total, carried), "col", 1)
            left, left_index = shifted((left, left_index), "row", 1)
    return total[None, None]


def encode(parts, code_ref):
    rows = parts[0].shape[0]
    row = lax.broadcasted_iota(jnp.int32, (PAD, LANES), 0)
    scales = jnp.zeros((PAD, LANES), jnp.float32)
    for m, value in enumerate(parts):
        peak = jnp.maximum(jnp.max(jnp.abs(value), axis=0, keepdims=True), 2.0**-100)
        power = jnp.floor(jnp.log2(peak))
        shrink = jnp.exp2(-power)
        grains = jnp.ceil(peak * shrink * GRAIN) + 1.0
        factor = (TOP * GRAIN / grains) * shrink
        code_ref[m * rows : (m + 1) * rows] = jnp.round(value * factor).astype(jnp.int32).astype(jnp.int16)
        scales = jnp.where(row == m, power, jnp.where(row == PAD // 2 + m, grains, scales))
    code_ref[len(parts) * rows :] = scales.astype(jnp.int16)


def decoded(code_ref, rows):
    count = code_ref.shape[0] // rows
    tile = code_ref[count * rows :].astype(jnp.float32)
    scales = jnp.exp2(tile[: PAD // 2]) * (tile[PAD // 2 :] * (1.0 / (TOP * GRAIN)))
    for m in range(count):
        yield code_ref[m * rows : (m + 1) * rows].astype(jnp.float32) * scales[m : m + 1]


def spread_left(packed_ref, rows, half, dense_ref):
    side = lax.broadcasted_iota(jnp.int32, (1, LANES), 1) // half
    count = packed_ref.shape[0] // rows
    index = packed_ref[count * rows :].astype(jnp.float32)
    for i in range(rows // half):
        here, there, data, turned = [], [], [], []
        for b in range(count):
            column = index[i * count + b : i * count + b + 1].astype(jnp.int32)
            here.append(jnp.broadcast_to(column - side, (PAD, LANES)))
            there.append(jnp.broadcast_to(pltpu.roll(column, half, 1) - side, (PAD, LANES)))
            data.append(packed_ref[b * rows + i * half : b * rows + (i + 1) * half])
            turned.append(pltpu.roll(data[-1], half, 1))
        for m in range(dense_ref.shape[1] // LANES):
            masks = [(h == 2 * m, t == 2 * m) for h, t in zip(here, there)]
            for top in range(0, half, PAD):
                total = jnp.zeros((PAD, LANES), jnp.bfloat16)
                for b, (stays, turns) in enumerate(masks):
                    total = jnp.where(stays, data[b][top : top + PAD], total)
                    total = jnp.where(turns, turned[b][top : top + PAD], total)
                rows_of = slice(i * half + top, i * half + top + PAD)
                dense_ref[rows_of, m * LANES : (m + 1) * LANES] = total


def product(left, dense_ref):
    found = []
    for m in range(0, dense_ref.shape[0], 2):
        pair = jnp.concatenate([dense_ref[m], dense_ref[m + 1]], axis=1)
        part = jnp.dot(left, pair, preferred_element_type=jnp.float32)
        found += [part[:, :LANES], part[:, LANES:]]
    return found


def place(blocks, dense_ref):
    half = blocks[0][0].shape[0]
    side = lax.broadcasted_iota(jnp.int32, (half, LANES), 1) // half
    work = []
    for block, row, col in blocks:
        both = jnp.concatenate([block.astype(jnp.float32)]*2, axis=1).astype(jnp.bfloat16)
        at = (lax.shift_right_logical(col, 1), slice(row * half, (row + 1) * half))
        work.append((at, jnp.where(side == (col & 1), both, dense_ref[at])))
    for at, value in work:
        dense_ref[at] = value


def pack_kernel(cols_hbm, left_hbm, packed_ref, cols_ref, left_ref, sem):
    ib, nl, half, _ = left_ref.shape
    rows, count = ib * half, nl // 2
    copies = [pltpu.make_async_copy(cols_hbm, cols_ref, sem.at[ib])]
    for i in range(ib):
        copies.append(pltpu.make_async_copy(left_hbm.at[0, 0, i], left_ref.at[i], sem.at[i]))
    for copy in copies:
        copy.start()
    side = lax.broadcasted_iota(jnp.int32, (PAD, LANES), 1) // half
    row = lax.broadcasted_iota(jnp.int32, (PAD, LANES), 0)
    index = jnp.zeros((PAD, LANES), jnp.int32)
    copies[0].wait()
    for i in range(ib):
        for b in range(count):
            cols = jnp.where(side == 0, cols_ref[0, 0, i, 2 * b], cols_ref[0, 0, i, 2 * b + 1])
            index = jnp.where(row == i * count + b, cols, index)
    packed_ref[count * rows :] = index.astype(jnp.float32).astype(jnp.bfloat16)
    for i in range(ib):
        copies[1 + i].wait()
        for b in range(count):
            pair = jnp.concatenate([left_ref[i, 2 * b], left_ref[i, 2 * b + 1]], axis=1)
            packed_ref[b * rows + i * half : b * rows + (i + 1) * half] = pair


def first_kernel(
    cols_hbm, right_hbm, packed_ref, dense_ref, code_ref, left_ref, cols_ref, right_ref, sem
):
    kb, kept, half, _ = right_ref.shape
    rows = left_ref.shape[0]
    parts = sem.shape[0] - 1
    step = kb // parts
    pairs = [(cols_hbm, cols_ref)]
    for part in range(parts):
        here = pl.ds(part * step, step)
        pairs.append((right_hbm.at[0, 0, here], right_ref.at[here]))
    copies = [pltpu.make_async_copy(*pair, sem.at[n]) for n, pair in enumerate(pairs)]
    for copy in copies:
        copy.start()
    dense_ref[...] = jnp.zeros_like(dense_ref)
    spread_left(packed_ref, rows, half, left_ref)
    copies[0].wait()
    for part in range(parts):
        copies[part + 1].wait()
        for e in range(kept):
            ks = range(part * step, (part + 1) * step)
            place([(right_ref[k, e], k, cols_ref[0, e, 0, k]) for k in ks], dense_ref)
    encode(product(left_ref[...], dense_ref), code_ref)


def second_kernel(half, dense_ref, packed_ref, code_ref, left_ref):
    spread_left(packed_ref, left_ref.shape[0], half, left_ref)
    encode(product(left_ref[...], dense_ref), code_ref)


def swapped():
    return (lax.axis_index("col") + lax.axis_index("row")) % 2


def kept_kernel(half, dense_ref, near_ref, far_ref, kept_ref, left_ref):
    _, _, rows, _ = kept_ref.shape
    spread_left(near_ref, rows, half, left_ref.at[:rows])
    spread_left(far_ref, rows, half, left_ref.at[rows:])
    slot = swapped()
    for m, part in enumerate(product(left_ref[...], dense_ref)):
        kept_ref[slot, m] = part[:rows]
        kept_ref[1 - slot, m] = part[rows:]


def sum_kernel(half, odd, own_ref, one_ref, far_ref, kept_ref, code_ref, *refs):
    if odd:
        held_ref, a_ref, b_ref, keep_ref, wide_ref, new_ref = refs
    else:
        a_ref, new_ref, wide_ref = refs
    _, pairs, rows, _ = kept_ref.shape
    for m, part in enumerate(decoded(code_ref, rows)):
        total = kept_ref[odd, m] + part
        wide_ref[m] = total
        wide_ref[pairs + m] = pltpu.roll(total, half, 1)
    low = lax.broadcasted_iota(jnp.int32, (half, LANES), 1) < half
    stays = (lax.axis_index("col") % 2) == odd

    def pick(near, i, o):
        picked = []
        for side in range(2):
            at = (0, 0, i, o + side)
            j = jnp.where(stays, own_ref[at], one_ref[at]) if near else far_ref[at]
            slot = lax.shift_right_logical(j, 1) + pairs * ((j + side) & 1)
            picked.append(wide_ref[slot, i * half : (i + 1) * half, :])
        return jnp.where(low, picked[0], picked[1])

    for near, target in ((False, a_ref), (True, new_ref)):
        steps = range(0, own_ref.shape[3], 2)
        encode([jnp.concatenate([pick(near, i, o) for i in range(rows // half)], axis=0) for o in steps], target)
    if odd:
        b_ref[...] = jnp.where(stays, held_ref[...], new_ref[...])
        keep_ref[...] = jnp.where(stays, new_ref[...], held_ref[...])


def last_kernel(half, a_ref, b_ref, c_ref, own_ref, out_hbm, out_ref, sem):
    ib = out_ref.shape[0]
    arrived = [decoded(ref, ib * half) for ref in (a_ref, b_ref, c_ref, own_ref)]
    copies = []
    for m, (a, b, c, own) in enumerate(zip(*arrived)):
        total = (a + own) + (b + c)
        for i in range(ib):
            part = total[i * half : (i + 1) * half]
            out_ref[i, 2 * m] = part[:, :half]
            out_ref[i, 2 * m + 1] = part[:, half:]
            here = pl.ds(2 * m, 2)
            copies.append(pltpu.make_async_copy(out_ref.at[i, here], out_hbm.at[0, 0, i, here], sem.at[m * ib + i]))
            copies[-1].start()
    for copy in copies:
        copy.wait()


VMEM = pl.BlockSpec(memory_space=pltpu.VMEM)
SMEM = pl.BlockSpec(memory_space=pltpu.SMEM)
HBM = pl.BlockSpec(memory_space=pltpu.HBM)
PARTS = 4
COST = pl.CostEstimate(flops=2000000000, bytes_accessed=20000000, transcendentals=0)
PARAMS = pltpu.CompilerParams(vmem_limit_bytes=40 * 2**20)


def grid_path(n_row, n_col, left_blocks, left_cols, right_blocks, right_cols, out_cols):
    _, _, ib, nl, bs, _ = left_blocks.shape
    kb = right_blocks.shape[2]
    jb = kb
    no = out_cols.shape[3]
    rows = ib * bs

    def send(value, to):
        pairs = []
        for r in range(n_row):
            for c in range(n_col):
                target = to(r, c)
                pairs.append((r * n_col + c, target[0] * n_col + target[1]))
        return lax.ppermute(value, ("row", "col"), pairs)

    def along(even, odd):
        return lambda r, c: (r, c ^ (2 * (odd if c % 2 else even)))

    wide_cols, no_cols = jb * bs // LANES, no * bs // LANES
    code = jax.ShapeDtypeStruct((wide_cols * rows + PAD, LANES), jnp.int16)
    small = jax.ShapeDtypeStruct((no_cols * rows + PAD, LANES), jnp.int16)
    both = jax.ShapeDtypeStruct((2, wide_cols, rows, LANES), jnp.float32)
    left_scratch = pltpu.VMEM((rows, kb * bs), jnp.bfloat16)
    def in_hbm(*arrays):
        return [pltpu.with_memory_space_constraint(array, pltpu.HBM) for array in arrays]

    packed = pl.pallas_call(
        pack_kernel,
        out_shape=jax.ShapeDtypeStruct((nl * bs // LANES * rows + PAD, LANES), jnp.bfloat16),
        in_specs=[HBM] * 2,
        out_specs=VMEM,
        scratch_shapes=[
            pltpu.SMEM(left_cols.shape[:2] + (ib, nl), jnp.int32),
            pltpu.VMEM(left_blocks.shape[2:], jnp.bfloat16),
            pltpu.SemaphoreType.DMA((ib + 1,)),
        ],
        compiler_params=PARAMS,
        name="pack",
    )(*in_hbm(left_cols, left_blocks))
    far_cols = (send(out_cols, along(2, 3)), send(out_cols, along(3, 2)))
    one_cols = send(out_cols, along(1, 1))
    dense, code_one = pl.pallas_call(
        first_kernel,
        out_shape=(
            jax.ShapeDtypeStruct((wide_cols, kb * bs, LANES), jnp.bfloat16),
            code,
        ),
        in_specs=[HBM, HBM, VMEM],
        out_specs=(VMEM, VMEM),
        scratch_shapes=[
            left_scratch,
            pltpu.SMEM((1, right_cols.shape[3], 1, kb), jnp.int32),
            pltpu.VMEM(right_blocks.shape[2:], jnp.bfloat16),
            pltpu.SemaphoreType.DMA((PARTS + 1,)),
        ],
        compiler_params=PARAMS,
        name="first",
    )(*in_hbm(right_cols.transpose(0, 3, 1, 2), right_blocks), packed)
    got_one = send(code_one, lambda r, c: (r, c ^ 1))
    across = send(packed, lambda r, c: ((r + 2) % n_row, c))
    dense, packed = lax.optimization_barrier((dense, packed))
    near = send(packed, lambda r, c: (r ^ 1, c))
    far = send(across, lambda r, c: (r ^ 1, c))
    code_two = pl.pallas_call(
        functools.partial(second_kernel, bs),
        out_shape=code,
        in_specs=[VMEM] * 2,
        out_specs=VMEM,
        scratch_shapes=[left_scratch],
        compiler_params=PARAMS,
        name="second",
    )(dense, across)
    got_two = send(code_two, lambda r, c: (r, c ^ 1))
    kept = pl.pallas_call(
        functools.partial(kept_kernel, bs),
        out_shape=both,
        in_specs=[VMEM] * 3,
        out_specs=VMEM,
        scratch_shapes=[pltpu.VMEM((2 * rows, kb * bs), jnp.bfloat16)],
        compiler_params=PARAMS,
        name="kept",
    )(dense, near, far)

    def summed(odd, code, *held):
        scratch = [pltpu.VMEM((2 * wide_cols, rows, LANES), jnp.float32)]
        scratch += odd * [pltpu.VMEM(small.shape, small.dtype)]
        return pl.pallas_call(
            functools.partial(sum_kernel, bs, odd),
            out_shape=(2 + odd) * (small,),
            in_specs=[SMEM] * 3 + [VMEM] * (2 + odd),
            out_specs=(2 + odd) * (VMEM,),
            scratch_shapes=scratch,
            compiler_params=PARAMS,
            cost_estimate=None if odd else COST,
            name="sum",
        )(out_cols, one_cols, far_cols[odd], kept, code, *held)

    a, held = summed(0, got_one)
    got = [send(a, along(2, 3))]
    a, b, own = summed(1, got_two, held)
    last = send(b, along(1, 1))
    got += [send(a, along(3, 2)), last, own]
    return pl.pallas_call(
        functools.partial(last_kernel, bs),
        out_shape=jax.ShapeDtypeStruct((1, 1, ib, no, bs, bs), jnp.float32),
        in_specs=[VMEM] * len(got),
        out_specs=HBM,
        scratch_shapes=[
            pltpu.VMEM((ib, no, bs, bs), jnp.float32),
            pltpu.SemaphoreType.DMA((ib * no // 2,)),
        ],
        compiler_params=PARAMS,
        name="last",
    )(*got)


def solution(mesh):
    in_specs = (
        P("row", "col", None, None, None, None),
        P("row", "col", None, None),
        P("row", "col", None, None, None, None),
        P("row", "col", None, None),
        P("row", "col", None, None),
    )
    out_specs = P("row", "col", None, None, None, None)
    n_row, n_col = mesh.shape["row"], mesh.shape["col"]
    body = functools.partial(grid_path, n_row, n_col) if (n_row, n_col) == (4, TICKS) else ring
    return jax.shard_map(body, mesh=mesh, in_specs=in_specs, out_specs=out_specs, check_vma=False)
```

```python
import functools

import jax
import jax.numpy as jnp
from jax import lax
from jax.experimental import pallas as pl
from jax.experimental.pallas import tpu as pltpu
from jax.sharding import PartitionSpec as P

TICKS = 8
LANES = 128
PAD = 16
TOP = 32767.0
GRAIN = 8192.0


def shifted(value, axis, steps):
    count = lax.axis_size(axis)
    pairs = [(source, (source + steps) % count) for source in range(count)]
    return lax.ppermute(value, axis, pairs)


def one_tick(left, left_cols, right, right_cols, pattern):
    inner = right.shape[0]
    pick_row = (left_cols[:, :, None] == jnp.arange(inner, dtype=jnp.int32)[None, None, :]).astype(
        jnp.float32
    )
    match = (right_cols[None, None, :, :] == pattern[:, :, None, None]).astype(jnp.float32)
    select = jnp.einsum("iak,iokb->iaokb", pick_row, match).astype(jnp.bfloat16)
    chosen = jnp.einsum(
        "iaokb,kbyz->iaoyz", select, right, preferred_element_type=jnp.float32
    ).astype(jnp.bfloat16)
    return jnp.einsum("iaxy,iaoyz->ioxz", left, chosen, preferred_element_type=jnp.float32)


def ring(left_blocks, left_cols, right_blocks, right_cols, out_cols):
    left = left_blocks[0, 0]
    left_index = left_cols[0, 0]
    right = right_blocks[0, 0]
    right_index = right_cols[0, 0]
    pattern = out_cols[0, 0]
    total = jnp.zeros((left.shape[0], pattern.shape[1], left.shape[2], left.shape[3]), jnp.float32)
    carried = shifted(pattern, "col", 1 - TICKS)
    for step in range(TICKS):
        total = total + one_tick(left, left_index, right, right_index, carried)
        if step + 1 < TICKS:
            total, carried = shifted((total, carried), "col", 1)
            left, left_index = shifted((left, left_index), "row", 1)
    return total[None, None]


def encode(parts, code_ref):
    rows = parts[0].shape[0]
    row = lax.broadcasted_iota(jnp.int32, (PAD, LANES), 0)
    scales = jnp.zeros((PAD, LANES), jnp.float32)
    for m, value in enumerate(parts):
        peak = jnp.maximum(jnp.max(jnp.abs(value), axis=0, keepdims=True), 2.0**-100)
        power = jnp.floor(jnp.log2(peak))
        shrink = jnp.exp2(-power)
        grains = jnp.ceil(peak * shrink * GRAIN) + 1.0
        factor = (TOP * GRAIN / grains) * shrink
        code_ref[m * rows : (m + 1) * rows] = jnp.round(value * factor).astype(jnp.int32).astype(jnp.int16)
        scales = jnp.where(row == m, power, jnp.where(row == PAD // 2 + m, grains, scales))
    code_ref[len(parts) * rows :] = scales.astype(jnp.int16)


def decoded(code_ref, rows):
    count = code_ref.shape[0] // rows
    tile = code_ref[count * rows :].astype(jnp.float32)
    scales = jnp.exp2(tile[: PAD // 2]) * (tile[PAD // 2 :] * (1.0 / (TOP * GRAIN)))
    for m in range(count):
        yield code_ref[m * rows : (m + 1) * rows].astype(jnp.float32) * scales[m : m + 1]


def spread_left(packed_ref, rows, half, dense_ref):
    side = lax.broadcasted_iota(jnp.int32, (1, LANES), 1) // half
    count = packed_ref.shape[0] // rows
    index = packed_ref[count * rows :].astype(jnp.float32)
    for i in range(rows // half):
        here, there, data, turned = [], [], [], []
        for b in range(count):
            column = index[i * count + b : i * count + b + 1].astype(jnp.int32)
            here.append(jnp.broadcast_to(column - side, (PAD, LANES)))
            there.append(jnp.broadcast_to(pltpu.roll(column, half, 1) - side, (PAD, LANES)))
            data.append(packed_ref[b * rows + i * half : b * rows + (i + 1) * half])
            turned.append(pltpu.roll(data[-1], half, 1))
        for m in range(dense_ref.shape[1] // LANES):
            masks = [(h == 2 * m, t == 2 * m) for h, t in zip(here, there)]
            for top in range(0, half, PAD):
                total = jnp.zeros((PAD, LANES), jnp.bfloat16)
                for b, (stays, turns) in enumerate(masks):
                    total = jnp.where(stays, data[b][top : top + PAD], total)
                    total = jnp.where(turns, turned[b][top : top + PAD], total)
                rows_of = slice(i * half + top, i * half + top + PAD)
                dense_ref[rows_of, m * LANES : (m + 1) * LANES] = total


def product(left, dense_ref):
    found = []
    for m in range(0, dense_ref.shape[0], 2):
        pair = jnp.concatenate([dense_ref[m], dense_ref[m + 1]], axis=1)
        part = jnp.dot(left, pair, preferred_element_type=jnp.float32)
        found += [part[:, :LANES], part[:, LANES:]]
    return found


def place(blocks, dense_ref):
    half = blocks[0][0].shape[0]
    side = lax.broadcasted_iota(jnp.int32, (half, LANES), 1) // half
    work = []
    for block, row, col in blocks:
        both = jnp.concatenate([block.astype(jnp.float32)]*2, axis=1).astype(jnp.bfloat16)
        at = (lax.shift_right_logical(col, 1), slice(row * half, (row + 1) * half))
        work.append((at, jnp.where(side == (col & 1), both, dense_ref[at])))
    for at, value in work:
        dense_ref[at] = value


def pack_kernel(cols_hbm, left_hbm, packed_ref, cols_ref, left_ref, sem):
    ib, nl, half, _ = left_ref.shape
    rows, count = ib * half, nl // 2
    copies = [pltpu.make_async_copy(cols_hbm, cols_ref, sem.at[ib])]
    for i in range(ib):
        copies.append(pltpu.make_async_copy(left_hbm.at[0, 0, i], left_ref.at[i], sem.at[i]))
    for copy in copies:
        copy.start()
    side = lax.broadcasted_iota(jnp.int32, (PAD, LANES), 1) // half
    row = lax.broadcasted_iota(jnp.int32, (PAD, LANES), 0)
    index = jnp.zeros((PAD, LANES), jnp.int32)
    copies[0].wait()
    for i in range(ib):
        for b in range(count):
            cols = jnp.where(side == 0, cols_ref[0, 0, i, 2 * b], cols_ref[0, 0, i, 2 * b + 1])
            index = jnp.where(row == i * count + b, cols, index)
    packed_ref[count * rows :] = index.astype(jnp.float32).astype(jnp.bfloat16)
    for i in range(ib):
        copies[1 + i].wait()
        for b in range(count):
            pair = jnp.concatenate([left_ref[i, 2 * b], left_ref[i, 2 * b + 1]], axis=1)
            packed_ref[b * rows + i * half : b * rows + (i + 1) * half] = pair


def first_kernel(
    cols_hbm, right_hbm, packed_ref, dense_ref, code_ref, left_ref, cols_ref, right_ref, sem
):
    kb, kept, half, _ = right_ref.shape
    rows = left_ref.shape[0]
    parts = sem.shape[0] - 1
    step = kb // parts
    pairs = [(cols_hbm, cols_ref)]
    for part in range(parts):
        here = pl.ds(part * step, step)
        pairs.append((right_hbm.at[0, 0, here], right_ref.at[here]))
    copies = [pltpu.make_async_copy(*pair, sem.at[n]) for n, pair in enumerate(pairs)]
    for copy in copies:
        copy.start()
    dense_ref[...] = jnp.zeros_like(dense_ref)
    spread_left(packed_ref, rows, half, left_ref)
    copies[0].wait()
    for part in range(parts):
        copies[part + 1].wait()
        for e in range(kept):
            ks = range(part * step, (part + 1) * step)
            place([(right_ref[k, e], k, cols_ref[0, e, 0, k]) for k in ks], dense_ref)
    encode(product(left_ref[...], dense_ref), code_ref)


def second_kernel(half, dense_ref, packed_ref, code_ref, left_ref):
    spread_left(packed_ref, left_ref.shape[0], half, left_ref)
    encode(product(left_ref[...], dense_ref), code_ref)


def swapped():
    return (lax.axis_index("col") + lax.axis_index("row")) % 2


def kept_kernel(half, dense_ref, near_ref, far_ref, kept_ref, left_ref):
    _, _, rows, _ = kept_ref.shape
    spread_left(near_ref, rows, half, left_ref.at[:rows])
    spread_left(far_ref, rows, half, left_ref.at[rows:])
    slot = swapped()
    for m, part in enumerate(product(left_ref[...], dense_ref)):
        kept_ref[slot, m] = part[:rows]
        kept_ref[1 - slot, m] = part[rows:]


def sum_kernel(half, odd, own_ref, one_ref, far_ref, kept_ref, code_ref, *refs):
    if odd:
        held_ref, a_ref, b_ref, keep_ref, wide_ref, new_ref = refs
    else:
        a_ref, new_ref, wide_ref = refs
    _, pairs, rows, _ = kept_ref.shape
    for m, part in enumerate(decoded(code_ref, rows)):
        total = kept_ref[odd, m] + part
        wide_ref[m] = total
        wide_ref[pairs + m] = pltpu.roll(total, half, 1)
    low = lax.broadcasted_iota(jnp.int32, (half, LANES), 1) < half
    stays = (lax.axis_index("col") % 2) == odd

    def pick(near, i, o):
        picked = []
        for side in range(2):
            at = (0, 0, i, o + side)
            j = jnp.where(stays, own_ref[at], one_ref[at]) if near else far_ref[at]
            slot = lax.shift_right_logical(j, 1) + pairs * ((j + side) & 1)
            picked.append(wide_ref[slot, i * half : (i + 1) * half, :])
        return jnp.where(low, picked[0], picked[1])

    for near, target in ((False, a_ref), (True, new_ref)):
        steps = range(0, own_ref.shape[3], 2)
        encode([jnp.concatenate([pick(near, i, o) for i in range(rows // half)], axis=0) for o in steps], target)
    if odd:
        b_ref[...] = jnp.where(stays, held_ref[...], new_ref[...])
        keep_ref[...] = jnp.where(stays, new_ref[...], held_ref[...])


def last_kernel(half, a_ref, b_ref, c_ref, own_ref, out_hbm, out_ref, sem):
    ib = out_ref.shape[0]
    arrived = [decoded(ref, ib * half) for ref in (a_ref, b_ref, c_ref, own_ref)]
    copies = []
    for m, (a, b, c, own) in enumerate(zip(*arrived)):
        total = (a + own) + (b + c)
        for i in range(ib):
            part = total[i * half : (i + 1) * half]
            out_ref[i, 2 * m] = part[:, :half]
            out_ref[i, 2 * m + 1] = part[:, half:]
            here = pl.ds(2 * m, 2)
            copies.append(pltpu.make_async_copy(out_ref.at[i, here], out_hbm.at[0, 0, i, here], sem.at[m * ib + i]))
            copies[-1].start()
    for copy in copies:
        copy.wait()


VMEM = pl.BlockSpec(memory_space=pltpu.VMEM)
SMEM = pl.BlockSpec(memory_space=pltpu.SMEM)
HBM = pl.BlockSpec(memory_space=pltpu.HBM)
PARTS = 2
COST = pl.CostEstimate(flops=2000000000, bytes_accessed=20000000, transcendentals=0)
PARAMS = pltpu.CompilerParams(vmem_limit_bytes=40 * 2**20)


def grid_path(n_row, n_col, left_blocks, left_cols, right_blocks, right_cols, out_cols):
    _, _, ib, nl, bs, _ = left_blocks.shape
    kb = right_blocks.shape[2]
    jb = kb
    no = out_cols.shape[3]
    rows = ib * bs

    def send(value, to):
        pairs = []
        for r in range(n_row):
            for c in range(n_col):
                target = to(r, c)
                pairs.append((r * n_col + c, target[0] * n_col + target[1]))
        return lax.ppermute(value, ("row", "col"), pairs)

    def along(even, odd):
        return lambda r, c: (r, c ^ (2 * (odd if c % 2 else even)))

    wide_cols, no_cols = jb * bs // LANES, no * bs // LANES
    code = jax.ShapeDtypeStruct((wide_cols * rows + PAD, LANES), jnp.int16)
    small = jax.ShapeDtypeStruct((no_cols * rows + PAD, LANES), jnp.int16)
    both = jax.ShapeDtypeStruct((2, wide_cols, rows, LANES), jnp.float32)
    left_scratch = pltpu.VMEM((rows, kb * bs), jnp.bfloat16)
    def in_hbm(*arrays):
        return [pltpu.with_memory_space_constraint(array, pltpu.HBM) for array in arrays]

    packed = pl.pallas_call(
        pack_kernel,
        out_shape=jax.ShapeDtypeStruct((nl * bs // LANES * rows + PAD, LANES), jnp.bfloat16),
        in_specs=[HBM] * 2,
        out_specs=VMEM,
        scratch_shapes=[
            pltpu.SMEM(left_cols.shape[:2] + (ib, nl), jnp.int32),
            pltpu.VMEM(left_blocks.shape[2:], jnp.bfloat16),
            pltpu.SemaphoreType.DMA((ib + 1,)),
        ],
        compiler_params=PARAMS,
        name="pack",
    )(*in_hbm(left_cols, left_blocks))
    one_cols = send(out_cols, along(1, 1))
    dense, code_one = pl.pallas_call(
        first_kernel,
        out_shape=(
            jax.ShapeDtypeStruct((wide_cols, kb * bs, LANES), jnp.bfloat16),
            code,
        ),
        in_specs=[HBM, HBM, VMEM],
        out_specs=(VMEM, VMEM),
        scratch_shapes=[
            left_scratch,
            pltpu.SMEM((1, right_cols.shape[3], 1, kb), jnp.int32),
            pltpu.VMEM(right_blocks.shape[2:], jnp.bfloat16),
            pltpu.SemaphoreType.DMA((PARTS + 1,)),
        ],
        compiler_params=PARAMS,
        name="first",
    )(*in_hbm(right_cols.transpose(0, 3, 1, 2), right_blocks), packed)
    got_one = send(code_one, lambda r, c: (r, c ^ 1))
    across = send(packed, lambda r, c: ((r + 2) % n_row, c))
    dense, packed = lax.optimization_barrier((dense, packed))
    near = send(packed, lambda r, c: (r ^ 1, c))
    far = send(across, lambda r, c: (r ^ 1, c))
    code_two = pl.pallas_call(
        functools.partial(second_kernel, bs),
        out_shape=code,
        in_specs=[VMEM] * 2,
        out_specs=VMEM,
        scratch_shapes=[left_scratch],
        compiler_params=PARAMS,
        name="second",
    )(dense, across)
    far_cols = (send(out_cols, along(2, 3)), send(out_cols, along(3, 2)))
    got_two = send(code_two, lambda r, c: (r, c ^ 1))
    kept = pl.pallas_call(
        functools.partial(kept_kernel, bs),
        out_shape=both,
        in_specs=[VMEM] * 3,
        out_specs=VMEM,
        scratch_shapes=[pltpu.VMEM((2 * rows, kb * bs), jnp.bfloat16)],
        compiler_params=PARAMS,
        name="kept",
    )(dense, near, far)

    def summed(odd, code, *held):
        scratch = [pltpu.VMEM((2 * wide_cols, rows, LANES), jnp.float32)]
        scratch += odd * [pltpu.VMEM(small.shape, small.dtype)]
        return pl.pallas_call(
            functools.partial(sum_kernel, bs, odd),
            out_shape=(2 + odd) * (small,),
            in_specs=[SMEM] * 3 + [VMEM] * (2 + odd),
            out_specs=(2 + odd) * (VMEM,),
            scratch_shapes=scratch,
            compiler_params=PARAMS,
            cost_estimate=None if odd else COST,
            name="sum",
        )(out_cols, one_cols, far_cols[odd], kept, code, *held)

    a, held = summed(0, got_one)
    got = [send(a, along(2, 3))]
    a, b, own = summed(1, got_two, held)
    got += [send(a, along(3, 2)), send(b, along(1, 1)), own]
    return pl.pallas_call(
        functools.partial(last_kernel, bs),
        out_shape=jax.ShapeDtypeStruct((1, 1, ib, no, bs, bs), jnp.float32),
        in_specs=[VMEM] * len(got),
        out_specs=HBM,
        scratch_shapes=[
            pltpu.VMEM((ib, no, bs, bs), jnp.float32),
            pltpu.SemaphoreType.DMA((ib * no // 2,)),
        ],
        compiler_params=PARAMS,
        name="last",
    )(*got)


def solution(mesh):
    in_specs = (
        P("row", "col", None, None, None, None),
        P("row", "col", None, None),
        P("row", "col", None, None, None, None),
        P("row", "col", None, None),
        P("row", "col", None, None),
    )
    out_specs = P("row", "col", None, None, None, None)
    n_row, n_col = mesh.shape["row"], mesh.shape["col"]
    body = functools.partial(grid_path, n_row, n_col) if (n_row, n_col) == (4, TICKS) else ring
    return jax.shard_map(body, mesh=mesh, in_specs=in_specs, out_specs=out_specs, check_vma=False)
```
